256 devices in a mesh: dp: 2 (over z_lo), bricks: 128 (over z_hi, x, y, core).
Axes of the slice: x: 4, y: 4, z: 8 (z_hi: 4, z_lo: 2; z = z_hi * 2 + z_lo), core: 2. Of those that a mesh axis runs over, the one named last changes fastest.
Arguments:
- features: bfloat16 [2, 256, 512, 256], P('dp', 'bricks'), may hold values from -6 to 6
- active: int32 [2, 256, 512], P('dp', 'bricks'), may hold values from 0 to 1, as said below
- neighbours: int32 [2, 256, 27], P('dp', 'bricks'), may hold values from -1 to 255, as said below
- cond: bfloat16 [2, 256, 256], P('dp', 'bricks'), may hold values from -6 to 6
- gamma: float32 [256], replicated, may hold values from 0.1 to 1.9
- beta: float32 [256], replicated, may hold values from -3 to 3
- weight: bfloat16 [27, 256, 256], replicated, may hold values from -0.109375 to 0.109375
- cotangent: bfloat16 [2, 256, 512, 256], P('dp', 'bricks'), may hold values from -6 to 6
Outputs:
- output: bfloat16 [2, 256, 512, 256], P('dp', 'bricks')
- feature_grad: bfloat16 [2, 256, 512, 256], P('dp', 'bricks')
- weight_grad: float32 [1769472], P(('dp', 'bricks'))
The draws below stay inside these ranges and needn't reach their ends.
Inputs may be any that keep to these rules, and one draw needn't show every extreme that they name: Active voxels lie only in bricks that are present; a present brick's voxels are active at one of three densities; absent bricks have no active voxels. `neighbours`: bricks form a column two bricks wide and high, 64 layers long, four slots a layer in a drawn order; an entry is the global slot index of the present brick one step away in that direction, -1 where there is none; entry 13 is the brick itself or -1 if it is absent; the relation is symmetric under reversing the direction; every neighbour's slot lies on a device whose bricks index differs by at most 3, and that distance is reached.
All inputs are finite; a program needn't handle non-finite values.
Results may differ from the reference program's by a relative error of at most 0.0033.
Values may be sent and summed in bfloat16 or wider, within the bound.
A program may use at most 128 MiB of HBM per device.

```python
import jax
import jax.numpy as jnp
from jax import lax

C = 256
GROUPS = 32
BRICK = 8
SAMPLES = 2
BRICKS_ALL = 256


def brick_layout(key, layers):
    perm_key = jax.random.fold_in(key, 101)
    scores = jax.random.randint(perm_key, (layers, 4), 0, 1000) * 4 + jnp.arange(4, dtype=jnp.int32)[None, :]
    position = jnp.argsort(scores, axis=1).astype(jnp.int32)
    inverse = jnp.argsort(position, axis=1).astype(jnp.int32)
    keep_key = jax.random.fold_in(key, 102)
    present = jax.random.randint(keep_key, (layers, 4), 0, 4) > 0
    present = jnp.where(jnp.arange(layers)[:, None] < 2, True, present)
    return (position, inverse, present)


def sample_neighbours(position, inverse, present):
    layers = position.shape[0]
    layer_ids = jnp.arange(layers, dtype=jnp.int32)[:, None]
    coord_y = position // 2
    coord_z = position % 2
    entries = []
    for step_x in (-1, 0, 1):
        for step_y in (-1, 0, 1):
            for step_z in (-1, 0, 1):
                target_x = layer_ids + step_x + 0 * coord_y
                target_y = coord_y + step_y
                target_z = coord_z + step_z
                inside = (target_x >= 0) & (target_x < layers) & (target_y >= 0) & (target_y < 2) & (target_z >= 0) & (target_z < 2)
                clip_x = jnp.clip(target_x, 0, layers - 1)
                target_q = jnp.clip(target_y, 0, 1) * 2 + jnp.clip(target_z, 0, 1)
                target_j = jnp.take_along_axis(inverse[clip_x[:, 0]], target_q, axis=1)
                there = jnp.take_along_axis(present[clip_x[:, 0]], target_j, axis=1)
                valid = inside & present & there
                entries.append(jnp.where(valid, 4 * clip_x + target_j, -1))
    return jnp.stack(entries, axis=-1).reshape(layers * 4, 27)


def draw_neighbours(key, part):
    shared = key
    per_sample = []
    for sample in range(SAMPLES):
        position, inverse, present = brick_layout(jax.random.fold_in(shared, 1000 + sample), BRICKS_ALL // 4)
        per_sample.append(sample_neighbours(position, inverse, present))
    return jnp.stack(per_sample).astype(jnp.int32)


def draw_active(key, part):
    shared = key
    key = jax.random.fold_in(key, 5)
    per_sample = []
    for sample in range(SAMPLES):
        position, inverse, present = brick_layout(jax.random.fold_in(shared, 1000 + sample), BRICKS_ALL // 4)
        density = jax.random.randint(jax.random.fold_in(key, sample), (BRICKS_ALL, 1), 1, 4)
        voxel_bits = jax.random.randint(jax.random.fold_in(key, 50 + sample), (BRICKS_ALL, BRICK ** 3), 0, 4)
        alive = (voxel_bits < density) & present.reshape(BRICKS_ALL, 1)
        per_sample.append(alive.astype(jnp.int32))
    return jnp.stack(per_sample).astype(jnp.int32)


def group_offsets(key, lower, upper):
    sign_key = jax.random.fold_in(key, 11)
    size_key = jax.random.fold_in(key, 12)
    signs = (jax.random.randint(sign_key, (SAMPLES, 1, 1, GROUPS), 0, 2) * 2 - 1).astype(jnp.float32)
    magnitude = jax.random.uniform(size_key, (SAMPLES, 1, 1, GROUPS), jnp.float32, lower, upper)
    return jnp.repeat(signs * magnitude, C // GROUPS, axis=3)


def paired_offsets(key, lower, upper):
    sign_key = jax.random.fold_in(key, 13)
    size_key = jax.random.fold_in(key, 14)
    signs = (jax.random.randint(sign_key, (1, 1, 1, GROUPS), 0, 2) * 2 - 1).astype(jnp.float32)
    magnitude = jax.random.uniform(size_key, (1, 1, 1, GROUPS), jnp.float32, lower, upper)
    turns = 1.0 - 2.0 * (jnp.arange(SAMPLES) % 2).astype(jnp.float32)
    return jnp.repeat(turns[:, None, None, None] * signs * magnitude, C // GROUPS, axis=3)


def rough_noise(key):
    noise_key = jax.random.fold_in(key, 21)
    shape = (SAMPLES, BRICKS_ALL, BRICK ** 3, C)
    return jax.random.normal(noise_key, shape, jnp.float32)


def draw_features(key, part):
    key = jax.random.fold_in(key, 7)
    noise = rough_noise(key)
    shift = group_offsets(jax.random.fold_in(key, 31), 0.75, 1.5)
    return jnp.clip(noise + shift, -6.0, 6.0).astype(jnp.bfloat16)


def draw_cotangent(key, part):
    key = jax.random.fold_in(key, 9)
    noise = rough_noise(key)
    shift = paired_offsets(jax.random.fold_in(key, 41), 0.75, 1.5)
    return jnp.clip(noise + shift, -6.0, 6.0).astype(jnp.bfloat16)


def steps_of(key, extent, cuts, least, largest):
    loudness = 1.0
    for dim, parts in cuts:
        steps = jax.random.uniform(jax.random.fold_in(jax.random.fold_in(key, 6), dim), (parts,), jnp.float32, least / len(cuts), largest / len(cuts))
        loudness = loudness * jnp.repeat(jnp.exp(steps), extent[dim] // parts).reshape((-1,) + (1,) * (len(extent) - 1 - dim))
    return loudness


def gaussian(rng, shape, spread, bound, pieces=(), kind=jnp.bfloat16):
    level = steps_of(rng, shape, pieces, -0.22, 0.18) if pieces else 1.0
    drawn = jax.random.normal(rng, shape, jnp.float32) * spread * level
    return jnp.minimum(jnp.maximum(drawn, -bound), bound).astype(kind)


def setup_inputs(seed: int = 0) -> dict:
    seeds = jax.random.split(jax.random.key(seed), 9)
    features = draw_features(jax.random.fold_in(seeds[8], 71), 0)
    active = draw_active(jax.random.fold_in(seeds[8], 71), 0)
    neighbours = draw_neighbours(jax.random.fold_in(seeds[8], 71), 0)
    cond = gaussian(seeds[3], (SAMPLES, BRICKS_ALL, C), 1.0, 6.0, ((0, 2), (1, 128)))
    gamma = jnp.clip(1.0 + 0.18 * jax.random.normal(seeds[4], (C,), jnp.float32), 0.1, 1.9)
    beta = gaussian(seeds[5], (C,), 0.5, 3.0, (), jnp.float32)
    weight = gaussian(seeds[6], (27, C, C), (27 * C // 2) ** -0.5, 0.109375)
    cotangent = draw_cotangent(jax.random.fold_in(seeds[8], 71), 0)
    return dict(features=features, active=active, neighbours=neighbours, cond=cond, gamma=gamma, beta=beta, weight=weight, cotangent=cotangent)


EPSILON = 1e-05

def layer_span(step, width):
    if step == -1:
        return slice(width - 1, width)
    if step == 1:
        return slice(0, 1)
    return slice(0, width)

def brick_cut(block, step_x, step_y, step_z):
    width = block.shape[0]
    return block[layer_span(step_x, width), layer_span(step_y, width), layer_span(step_z, width)]

def assemble(table, nbr_row):
    planes = []
    for step_x in (-1, 0, 1):
        lines = []
        for step_y in (-1, 0, 1):
            cells = []
            for step_z in (-1, 0, 1):
                tap_index = (step_x + 1) * 9 + (step_y + 1) * 3 + (step_z + 1)
                target = nbr_row[tap_index]
                block = table[jnp.maximum(target, 0)]
                block = jnp.where(target >= 0, block, jnp.zeros_like(block))
                cells.append(brick_cut(block, step_x, step_y, step_z))
            lines.append(jnp.concatenate(cells, axis=2))
        planes.append(jnp.concatenate(lines, axis=1))
    return jnp.concatenate(planes, axis=0)

def columns(padded, width):
    patches = []
    for tap_x in range(3):
        for tap_y in range(3):
            for tap_z in range(3):
                window = padded[tap_x:tap_x + width, tap_y:tap_y + width, tap_z:tap_z + width]
                patches.append(window.reshape(width ** 3, -1))
    return jnp.concatenate(patches, axis=1)

def one_sample(feats, active, nbr, cond, gamma, beta, w_fwd, w_back, cot):
    per_group = C // GROUPS
    count_bricks = feats.shape[0]
    mask_f = active.astype(jnp.float32)[..., None]
    values = feats.astype(jnp.float32)

    def group_total(array):
        return lax.optimization_barrier(jnp.sum(array.reshape(-1, GROUPS, per_group), axis=(0, 2)))
    active_count = jnp.sum(mask_f) * per_group
    group_mean = jnp.repeat(group_total(mask_f * values) / active_count, per_group)
    centred = values - group_mean
    group_var = group_total(mask_f * centred * centred) / active_count
    inv_std = jnp.repeat(lax.rsqrt(group_var + EPSILON), per_group)
    x_hat = centred * inv_std
    pre_act = x_hat * gamma + beta + cond.astype(jnp.float32)[:, None, :]
    sigma = jax.nn.sigmoid(pre_act)
    hidden = (mask_f * pre_act * sigma).astype(jnp.bfloat16)
    masked_cot = active.astype(jnp.bfloat16)[..., None] * cot
    h_table = hidden.reshape(count_bricks, BRICK, BRICK, BRICK, C)
    z_table = masked_cot.reshape(count_bricks, BRICK, BRICK, BRICK, C)

    def brick_step(total, brick_id):
        nbr_row = nbr[brick_id]
        patches = columns(assemble(h_table, nbr_row), BRICK)
        conv_out = jnp.dot(patches, w_fwd, preferred_element_type=jnp.float32)
        back_patches = columns(assemble(z_table, nbr_row), BRICK)
        hidden_grad = jnp.dot(back_patches, w_back, preferred_element_type=jnp.float32)
        w_grad = lax.dot_general(patches, masked_cot[brick_id], (((0,), (0,)), ((), ())), preferred_element_type=jnp.float32)
        return (total + w_grad, (conv_out, hidden_grad))
    total, (conv_out, hidden_grad) = lax.scan(brick_step, jnp.zeros((27 * C, C), jnp.float32), jnp.arange(count_bricks, dtype=jnp.int32))
    output = (mask_f * (values + conv_out)).astype(jnp.bfloat16)
    scaled_grad = gamma * mask_f * hidden_grad * sigma * (1.0 + pre_act * (1.0 - sigma))
    grad_mean = jnp.repeat(group_total(scaled_grad) / active_count, per_group)
    cross_mean = jnp.repeat(group_total(scaled_grad * x_hat) / active_count, per_group)
    feature_grad = mask_f * (inv_std * (scaled_grad - grad_mean - x_hat * cross_mean) + cot.astype(jnp.float32))
    return (output, feature_grad.astype(jnp.bfloat16), total)

def reference(features, active, neighbours, cond, gamma, beta, weight, cotangent):
    w_fwd = weight.reshape(27 * C, C)
    w_back = jnp.transpose(weight[::-1], (0, 2, 1)).reshape(27 * C, C)
    outputs = []
    grads = []
    weight_total = jnp.zeros((27 * C, C), jnp.float32)
    for sample in range(SAMPLES):
        output, feature_grad, w_grad = one_sample(features[sample], active[sample], neighbours[sample], cond[sample], gamma, beta, w_fwd, w_back, cotangent[sample])
        outputs.append(output)
        grads.append(feature_grad)
        weight_total = weight_total + w_grad
    return (jnp.stack(outputs), jnp.stack(grads), weight_total.reshape(-1))
```

```python
import functools

import jax
import jax.numpy as jnp
from jax import lax
from jax.experimental import pallas as pl
from jax.experimental.pallas import tpu as pltpu
from jax.sharding import PartitionSpec as P

MESH = pl.DeviceIdType.MESH
F32 = jnp.float32
BF16 = jnp.bfloat16
EPSILON = 1e-05
BIG = 1e30
LIMIT = 1e29
LAYERS = 64
ROWS = 3456
CUTS = (0, 4, 8, 11, 14)


def moved(index, stride, size, step):
    digit = (index // stride) % size
    return index + ((digit + step) % size - digit) * stride


def block_sum(v):
    return jnp.sum(v.reshape(v.shape[0] // 8, 8, v.shape[1]), axis=0)


def column_sum(v):
    return jnp.sum(v, axis=0, keepdims=True)


def packet(*rows):
    place = lax.broadcasted_iota(jnp.int32, (8, 256), 0)
    out = jnp.zeros((8, 256), F32)
    for i, row in enumerate(rows):
        out = jnp.where(place == i, row, out)
    return out


def pooled(parts):
    count = sum(p[2:3] for p in parts)
    first = sum(p[0:1] for p in parts)
    mean = first / jnp.maximum(count, 1.0)
    second = sum(p[1:2] for p in parts)
    for p in parts:
        apart = p[0:1] / jnp.maximum(p[2:3], 1.0) - mean
        second = second + p[2:3] * apart * apart
    return packet(first, second, count)


def group_sum(row):
    v = jnp.broadcast_to(row, (8, 256))
    lane = lax.broadcasted_iota(jnp.int32, (8, 256), 1)
    for step in (1, 2, 4):
        up = pltpu.roll(v, 256 - step, 1)
        down = pltpu.roll(v, step, 1)
        v = v + jnp.where((lane & step) == 0, up, down)
    return v[0:1]


def kernel(
    feat, cot, act, nbr, cond, gamma_in, beta_in, w_hbm,
    out, fgrad, wgrad,
    fs, zs, face_f, face_z, conds, conds_e, nbv, nbs,
    w_fwd, w_back, hz, zz, zt, wg, part, r1, r2, r3, r4, fin, fin_r,
    acc_f, acc_b, sg_s, outs, grads,
    own, got1, got2, got3, back1, back2, back3,
    w_sem, nb_sem, core_s, core_r, edge_s, edge_r, st_s, st_r, rs1_s, rs1_r, rs2_s, rs2_r, rs3_s, rs3_r, rs4_s, rs4_r,
    fin_s, fin_rs, res_s, res_r,
):
    d = lax.axis_index("dp")
    b = lax.axis_index("bricks")
    c = b % 2
    layer = b // 2
    xm = (b // 8) % 4
    ym = (b // 2) % 4
    hm = b // 32
    other = b + 1 - 2 * c
    after0 = ((layer + 1) % LAYERS) * 2
    before1 = ((layer + LAYERS - 1) % LAYERS) * 2 + 1
    beside = jnp.where(c == 0, (layer + LAYERS - 1) % LAYERS, (layer + 1) % LAYERS) * 2

    def copy(src, dst, ssem, rsem, dev):
        return pltpu.make_async_remote_copy(
            src_ref=src, dst_ref=dst, send_sem=ssem, recv_sem=rsem, device_id=dev, device_id_type=MESH
        )

    w_copy = pltpu.make_async_copy(w_hbm, w_fwd, w_sem)
    w_copy.start()

    barrier = pltpu.get_barrier_semaphore()
    partners = [{"bricks": moved(b, 1, 8, j)} for j in range(1, 8)]
    partners += [{"bricks": moved(b, 8, 4, j)} for j in range(1, 4)]
    partners += [{"bricks": moved(b, 32, 4, j)} for j in range(1, 4)]
    partners += [{"dp": 1 - d, "bricks": b}, {"dp": 1 - d, "bricks": other}]
    partners += [{"bricks": after0}, {"bricks": before1}, {"bricks": beside}, {"bricks": beside + 1}]
    for dev in partners:
        pl.semaphore_signal(barrier, inc=1, device_id=dev, device_id_type=MESH)

    rows = [act[s : s + 1, 128 * j : 128 * j + 128] for s in range(2) for j in range(4)]
    flags = jnp.concatenate(rows, axis=0).astype(F32)
    count = jnp.sum(jnp.sum(flags, axis=1, keepdims=True), axis=0, keepdims=True)
    flags_t = flags.T
    first = jnp.zeros((8, 256), F32)
    for s in range(2):
        for j in range(4):
            at = pl.ds(128 * j, 128)
            m = jnp.broadcast_to(flags_t[:, 4 * s + j : 4 * s + j + 1], (128, 256)) > 0.5
            f = feat[s, at, :].astype(F32)
            z = cot[s, at, :].astype(F32)
            fs[2 * c + s, at, :] = jnp.where(m, f, BIG).astype(BF16)
            zs[2 * c + s, at, :] = jnp.where(m, z, 0.0).astype(BF16)
            first = first + block_sum(jnp.where(m, f, 0.0))
    first = column_sum(first)
    local_mean = first / jnp.maximum(count, 1.0)
    second = jnp.zeros((8, 256), F32)
    for s in range(2):
        for j in range(4):
            f = fs[2 * c + s, pl.ds(128 * j, 128), :].astype(F32)
            apart = jnp.where(f < LIMIT, f - local_mean, 0.0)
            second = second + block_sum(apart * apart)
    second = column_sum(second)
    own[0] = packet(first, second, jnp.broadcast_to(count, (1, 256)))
    nbv[c] = jnp.zeros((8, 128), jnp.int32)
    nbv[c, 0:2, 0:27] = nbr[...]
    for s in range(2):
        conds[2 * c + s] = jnp.broadcast_to(cond[s : s + 1, :].astype(F32), (8, 256))
    pl.semaphore_wait(barrier, len(partners))

    def spread_start(stage, stride, size, boxes, base):
        sent = []
        for j in range(1, size):
            cp = copy(
                own.at[stage], boxes.at[j - 1], st_s.at[base + j - 1], st_r.at[base + j - 1],
                {"bricks": moved(b, stride, size, j)},
            )
            cp.start()
            sent.append(cp)
        return sent

    def spread_end(sent, stage, boxes):
        for cp in sent:
            cp.wait()
        return [own[stage]] + [boxes[j] for j in range(len(sent))]

    sent = spread_start(0, 1, 8, got1, 0)

    mine = pl.ds(2 * c, 2)
    core_copies = [
        copy(r.at[i], r.at[i], core_s.at[k], core_r.at[k], {"bricks": other})
        for k, (r, i) in enumerate(((nbv, c), (zs, mine), (fs, mine), (conds, mine)))
    ]
    for cp in core_copies:
        cp.start()
    edge_copies = []
    for k, (src, dst, up, down) in enumerate((
        (zs, face_z, pl.ds(448, 64), pl.ds(0, 64)),
        (fs, face_f, pl.ds(448, 64), pl.ds(0, 64)),
        (conds, conds_e, pl.ds(0, 8), pl.ds(0, 8)),
    )):
        for way, (at, dev) in enumerate(((up, after0), (down, before1))):
            cp = copy(
                src.at[mine, at], dst.at[mine], edge_s.at[2 * k + way], edge_r.at[k, c], {"bricks": dev}
            )
            cp.start()
            edge_copies.append(cp)

    def edge_wait(k, dst):
        for core in range(2):
            got = dst.at[pl.ds(2 * core, 2)]
            copy(got, got, edge_s.at[2 * k], edge_r.at[k, core], {"bricks": other}).wait_recv()

    for grid in (hz, zz):
        grid[:, 0:16, :] = jnp.zeros((10, 16, 768), BF16)
        grid[:, 272:288, :] = jnp.zeros((10, 16, 768), BF16)
    fs[4] = jnp.full((512, 256), BIG, BF16)
    zs[4] = jnp.zeros((512, 256), BF16)
    face_f[4] = jnp.full((64, 256), BIG, BF16)
    face_z[4] = jnp.zeros((64, 256), BF16)
    conds[4] = jnp.zeros((8, 256), F32)
    conds_e[4] = jnp.zeros((8, 256), F32)
    wg[pl.ds(128 + ROWS, 128), :] = jnp.zeros((128, 256), F32)

    w_copy.wait()

    def turn(g, carry):
        for e in range(3):
            w_back[g, pl.ds(256 * e, 256), :] = w_fwd[8 - g, pl.ds(256 * (2 - e), 256), :].T
        return carry

    lax.fori_loop(0, 9, turn, 0)

    merged = pooled(spread_end(sent, 0, got1))
    own[1] = merged
    sent = spread_start(1, 8, 4, got2, 7)

    core_copies[0].wait()
    nb_copy = pltpu.make_async_copy(nbv, nbs, nb_sem)
    nb_copy.start()
    nb_copy.wait()
    cy, cz, src, src_e = [], [], [], []
    here = []
    for j in range(4):
        def entry(k):
            return nbs[j // 2, j % 2, k]

        low_y = functools.reduce(jnp.maximum, [entry(9 * a + e) for a in range(3) for e in range(3)])
        low_z = functools.reduce(jnp.maximum, [entry(9 * a + 3 * e) for a in range(3) for e in range(3)])
        cy.append(jnp.where(low_y >= 0, 1, 0))
        cz.append(jnp.where(low_z >= 0, 1, 0))
        here.append(entry(13) >= 0)
    for q in range(4):
        qy, qz = q // 2, q % 2
        at, at_e = jnp.int32(4), jnp.int32(4)
        for j in range(4):
            at = jnp.where(here[j] & (cy[j] == qy) & (cz[j] == qz), j, at)
            t = nbs[j // 2, j % 2, 18 * c + 3 * (qy + 1 - cy[j]) + (qz + 1 - cz[j])]
            at_e = jnp.where(t >= 0, t & 3, at_e)
        src.append(at)
        src_e.append(at_e)

    zi = lax.broadcasted_iota(jnp.int32, (128, 256), 0) & 15

    def joined(left, right):
        pair = [v.reshape(8, 8, 256) for v in (left, right)]
        return jnp.concatenate(pair, axis=1).reshape(128, 256)

    def lay(grid, plane, half, v):
        at = pl.ds(16 + 128 * half, 128)
        grid[plane, at, 0:256] = jnp.where(zi == 0, 0.0, pltpu.roll(v, 1, 0)).astype(BF16)
        grid[plane, at, 256:512] = v.astype(BF16)
        grid[plane, at, 512:768] = jnp.where(zi == 15, 0.0, pltpu.roll(v, 127, 0)).astype(BF16)

    edge_plane = 9 * c

    core_copies[1].wait()
    edge_wait(0, face_z)

    def lay_z(x, carry):
        for half in range(2):
            at = pl.ds(pl.multiple_of(64 * x, 64), 64)
            v = joined(*[zs[src[2 * half + e], at, :].astype(F32) for e in range(2)])
            lay(zz, x + 1, half, v)
            zt[:, pl.ds(pl.multiple_of(256 * x + 128 * half, 128), 128)] = v.T.astype(BF16)
        return carry

    lax.fori_loop(0, 8, lay_z, 0)
    for half in range(2):
        lay(zz, edge_plane, half, joined(*[face_z[src_e[2 * half + e]].astype(F32) for e in range(2)]))

    merged = pooled(spread_end(sent, 1, got2))
    own[2] = merged
    sent = spread_start(2, 32, 4, got3, 10)

    def conv(grid, taps, acc, low, high):
        def step(g, carry):
            at = pl.ds(pl.multiple_of((g % 3) * 16, 16), 256)
            lhs = grid[pl.ds(4 * c + g // 3, 4), at, :].reshape(1024, 768)
            acc[...] += jnp.dot(lhs, taps[g], preferred_element_type=F32).reshape(4, 2, 8, 2, 8, 256)
            return carry

        lax.fori_loop(low, high, step, 0)

    acc_f[...] = jnp.zeros(acc_f.shape, F32)
    acc_b[...] = jnp.zeros(acc_b.shape, F32)
    conv(zz, w_back, acc_b, 0, 5)

    merged = pooled(spread_end(sent, 2, got3))
    total = merged[2:3]
    first, second = merged[0:1], merged[1:2]
    total_g = 8.0 * total
    mean = group_sum(first) / total_g
    apart = first / total - mean
    var = group_sum(second + total * apart * apart) / total_g
    inv_std = lax.rsqrt(var + EPSILON)
    gamma = gamma_in[...]
    beta = beta_in[...]
    slope = inv_std * gamma

    for cp in core_copies[2:]:
        cp.wait()
    edge_wait(1, face_f)
    edge_wait(2, conds_e)

    def activation(raw, shift):
        f = raw.astype(F32)
        m = f < LIMIT
        f = jnp.where(m, f, 0.0)
        apart = f - mean
        pre = apart * slope + (beta + shift[0:1])
        sigma = 1.0 / (1.0 + jnp.exp(-pre))
        return m, f, apart, pre, sigma

    def hidden(raw, shift):
        m, _, _, pre, sigma = activation(raw, shift)
        return jnp.where(m, pre * sigma, 0.0)

    def lay_h(x, carry):
        for half in range(2):
            at = pl.ds(pl.multiple_of(64 * x, 64), 64)
            slots = [src[2 * half + e] for e in range(2)]
            lay(hz, x + 1, half, joined(*[hidden(fs[j, at, :], conds[j]) for j in slots]))
        return carry

    lax.fori_loop(0, 8, lay_h, 0)
    for half in range(2):
        slots = [src_e[2 * half + e] for e in range(2)]
        lay(hz, edge_plane, half, joined(*[hidden(face_f[j], conds_e[j]) for j in slots]))

    def taps(low, high):
        def step(i, carry):
            t = 13 * c + i
            at = pl.ds(pl.multiple_of((t // 3) % 3 * 16, 16), 256)
            lanes = pl.ds(pl.multiple_of(t % 3 * 256, 256), 256)
            rhs = hz[pl.ds(t // 9, 8), at, lanes].reshape(2048, 256)
            made = jnp.dot(zt[...], rhs, preferred_element_type=F32)
            wg[pl.ds(pl.multiple_of(128 * (1 - c) + 256 * i, 128), 256), :] = made.T
            return carry

        lax.fori_loop(low, high, step, 0)

    way = ((8, 2), (2, 8))
    place = ((xm, ym), (ym, xm))

    def deal(h):
        def step(x, carry):
            base = pl.multiple_of(128 + 864 * h + 216 * x, 8)
            for y in range(4):
                low = 54 * y // 8 * 8
                v = wg[pl.ds(base + low, 64), :][54 * y - low : 54 * y - low + 56]
                part[0, x, h, y] = v[:, 0:128]
                part[1, y, h, x] = v[:, 128:256]
            return carry

        lax.fori_loop(0, 4, step, 0)

    live = {}

    def first_start(h):
        for k in range(2):
            a = place[k][0]
            for e, step in ((0, 1), (1, 3)):
                cp = copy(
                    part.at[k, (a + 2) % 4, h, pl.ds(2 * e, 2)], r1.at[k, h, e],
                    rs1_s.at[k, h, e], rs1_r.at[k, h, e], {"bricks": moved(b, way[k][0], 4, step)},
                )
                cp.start()
                live[1, k, h, e] = cp

    def second_start(h):
        for k in range(2):
            a = place[k][0]
            for e, step in ((0, 1), (1, 3)):
                live[1, k, h, e].wait()
                to = (a + step) % 4
                part[k, to, h, pl.ds(2 * e, 2)] += r1[k, h, e]
                cp = copy(
                    part.at[k, to, h], r2.at[k, h, e], rs2_s.at[k, h, e], rs2_r.at[k, h, e],
                    {"bricks": moved(b, way[k][0], 4, step)},
                )
                cp.start()
                live[2, k, h, e] = cp

    def third_start(h):
        for k in range(2):
            a, at = place[k]
            for e in range(2):
                live[2, k, h, e].wait()
            part[k, a, h] += r2[k, h, 0] + r2[k, h, 1]
            for j in range(1, 4):
                cp = copy(
                    part.at[k, a, h, (at + j) % 4], r3.at[k, h, j - 1], rs3_s.at[k, h, j - 1], rs3_r.at[k, h, j - 1],
                    {"bricks": moved(b, way[k][1], 4, j)},
                )
                cp.start()
                live[3, k, h, j] = cp

    def third_end(h):
        for k in range(2):
            a, at = place[k]
            for j in range(1, 4):
                live[3, k, h, j].wait()
            part[k, a, h, at] += r3[k, h, 0] + r3[k, h, 1] + r3[k, h, 2]

    def fourth_start():
        for k in range(2):
            a, at = place[k]
            for j in range(1, 4):
                cp = copy(
                    part.at[k, a, (hm + j) % 4, at], r4.at[k, j - 1], rs4_s.at[k, j - 1], rs4_r.at[k, j - 1],
                    {"bricks": moved(b, 32, 4, j)},
                )
                cp.start()
                live[4, k, j] = cp

    def fourth_end():
        for k in range(2):
            a, at = place[k]
            for j in range(1, 4):
                live[4, k, j].wait()
            fin[:, pl.ds(128 * k, 128)] = part[k, a, hm, at] + r4[k, 0] + r4[k, 1] + r4[k, 2]

    for h in range(4):
        taps(CUTS[h], CUTS[h + 1])
        deal(h)
        first_start(h)
        if h >= 2:
            second_start(h - 2)

    conv(zz, w_back, acc_b, 5, 9)
    second_start(2)

    def slot_block(j, plane):
        at = pl.ds(pl.multiple_of(256 * c + 64 * plane, 64), 64)
        return at, activation(fs[j, at, :], conds[j])

    def back_pass(plane, carry):
        one, two = carry
        for j in range(4):
            at, (m, f, apart, pre, sigma) = slot_block(j, plane)
            back = acc_b[plane, cy[j], :, cz[j]].reshape(64, 256)
            sg = jnp.where(m, gamma * back * sigma * (1.0 + pre * (1.0 - sigma)), 0.0)
            sg_s[j, plane] = sg
            one = one + block_sum(sg)
            two = two + block_sum(sg * (apart * inv_std))
        return one, two

    zero = jnp.zeros((8, 256), F32)
    one, two = lax.fori_loop(0, 4, back_pass, (zero, zero))
    own[3] = packet(column_sum(one), column_sum(two))
    sent = spread_start(3, 1, 8, back1, 13)
    second_start(3)
    conv(hz, w_fwd, acc_f, 0, 3)
    own[4] = sum(spread_end(sent, 3, back1))
    sent = spread_start(4, 8, 4, back2, 20)
    third_start(0)
    conv(hz, w_fwd, acc_f, 3, 6)
    own[5] = sum(spread_end(sent, 4, back2))
    sent = spread_start(5, 32, 4, back3, 23)
    third_start(1)
    conv(hz, w_fwd, acc_f, 6, 9)
    third_start(2)

    def out_pass(plane, carry):
        for j in range(4):
            at = pl.ds(pl.multiple_of(256 * c + 64 * plane, 64), 64)
            f = fs[j, at, :].astype(F32)
            made = acc_f[plane, cy[j], :, cz[j]].reshape(64, 256)
            outs[j, at, :] = jnp.where(f < LIMIT, f + made, 0.0).astype(BF16)
        return carry

    lax.fori_loop(0, 4, out_pass, 0)
    theirs = pl.ds(2 - 2 * c, 2)
    half_rows = pl.ds(pl.multiple_of(256 * c, 256), 256)

    def hand_over(ref, k):
        piece = ref.at[theirs, half_rows]
        cp = copy(piece, piece, res_s.at[k], res_r.at[k], {"bricks": other})
        cp.start()
        return cp

    out_copy = hand_over(outs, 0)
    third_end(0)
    sums = sum(spread_end(sent, 5, back3))
    grad_mean = group_sum(sums[0:1]) / total_g
    cross_mean = group_sum(sums[1:2]) / total_g
    third_end(1)
    third_start(3)

    def grad_pass(plane, carry):
        for j in range(4):
            at = pl.ds(pl.multiple_of(256 * c + 64 * plane, 64), 64)
            f = fs[j, at, :].astype(F32)
            x_hat = (f - mean) * inv_std
            v = inv_std * (sg_s[j, plane] - grad_mean - x_hat * cross_mean) + zs[j, at, :].astype(F32)
            grads[j, at, :] = jnp.where(f < LIMIT, v, 0.0).astype(BF16)
        return carry

    lax.fori_loop(0, 4, grad_pass, 0)
    grad_copy = hand_over(grads, 1)
    third_end(2)
    third_end(3)
    fourth_start()
    out_copy.wait()
    out[...] = outs[mine]
    grad_copy.wait()
    fgrad[...] = grads[mine]
    fourth_end()
    clique = [{"dp": 1 - d, "bricks": b}, {"dp": 1 - d, "bricks": other}, {"bricks": other}]
    last = []
    for k, dev in enumerate(clique):
        cp = copy(fin, fin_r.at[k], fin_s.at[k], fin_rs.at[k], dev)
        cp.start()
        last.append(cp)
    for cp in edge_copies:
        cp.wait_send()
    for cp in last:
        cp.wait()
    whole = jnp.where(c == d, fin[...] + fin_r[0], fin_r[1] + fin_r[2])
    wgrad[...] = jnp.where(c == 0, whole[0:27], whole[27:54])


def on_device(features, active, neighbours, cond, gamma, beta, weight, cotangent):
    vmem = pl.BlockSpec(memory_space=pltpu.VMEM)
    dma = pltpu.SemaphoreType.DMA
    scratch = [
        pltpu.VMEM((5, 512, 256), BF16),
        pltpu.VMEM((5, 512, 256), BF16),
        pltpu.VMEM((5, 64, 256), BF16),
        pltpu.VMEM((5, 64, 256), BF16),
        pltpu.VMEM((5, 8, 256), F32),
        pltpu.VMEM((5, 8, 256), F32),
        pltpu.VMEM((2, 8, 128), jnp.int32),
        pltpu.SMEM((2, 8, 128), jnp.int32),
        pltpu.VMEM((9, 768, 256), BF16),
        pltpu.VMEM((9, 768, 256), BF16),
        pltpu.VMEM((10, 288, 768), BF16),
        pltpu.VMEM((10, 288, 768), BF16),
        pltpu.VMEM((256, 2048), BF16),
        pltpu.VMEM((ROWS + 256, 256), F32),
        pltpu.VMEM((2, 4, 4, 4, 56, 128), F32),
        pltpu.VMEM((2, 4, 2, 2, 56, 128), F32),
        pltpu.VMEM((2, 4, 2, 4, 56, 128), F32),
        pltpu.VMEM((2, 4, 3, 56, 128), F32),
        pltpu.VMEM((2, 3, 56, 128), F32),
        pltpu.VMEM((56, 256), F32),
        pltpu.VMEM((3, 56, 256), F32),
        pltpu.VMEM((4, 2, 8, 2, 8, 256), F32),
        pltpu.VMEM((4, 2, 8, 2, 8, 256), F32),
        pltpu.VMEM((4, 4, 64, 256), F32),
        pltpu.VMEM((4, 512, 256), BF16),
        pltpu.VMEM((4, 512, 256), BF16),
        pltpu.VMEM((6, 8, 256), F32),
        pltpu.VMEM((7, 8, 256), F32),
        pltpu.VMEM((3, 8, 256), F32),
        pltpu.VMEM((3, 8, 256), F32),
        pltpu.VMEM((7, 8, 256), F32),
        pltpu.VMEM((3, 8, 256), F32),
        pltpu.VMEM((3, 8, 256), F32),
        dma, dma, dma((4,)), dma((4,)), dma((6,)), dma((3, 2)), dma((26,)), dma((26,)),
        dma((2, 4, 2)), dma((2, 4, 2)), dma((2, 4, 2)), dma((2, 4, 2)),
        dma((2, 4, 3)), dma((2, 4, 3)), dma((2, 3)), dma((2, 3)),
        dma((3,)), dma((3,)), dma((2,)), dma((2,)),
    ]
    output, feature_grad, weight_grad = pl.pallas_call(
        kernel,
        out_shape=(
            jax.ShapeDtypeStruct((2, 512, 256), BF16),
            jax.ShapeDtypeStruct((2, 512, 256), BF16),
            jax.ShapeDtypeStruct((27, 256), F32),
        ),
        in_specs=[vmem] * 7 + [pl.BlockSpec(memory_space=pl.ANY)],
        out_specs=(vmem, vmem, vmem),
        scratch_shapes=scratch,
        compiler_params=pltpu.CompilerParams(
            collective_id=0, has_side_effects=True, vmem_limit_bytes=60 * 2**20
        ),
        name="layer",
    )(
        features[0], cotangent[0], active[0], neighbours[0], cond[0],
        gamma.reshape(1, 256), beta.reshape(1, 256), weight.reshape(9, 768, 256),
    )
    return output[None], feature_grad[None], weight_grad.reshape(-1)


def solution(mesh):
    whole = P("dp", "bricks", None, None)
    rows = P("dp", "bricks", None)
    return jax.shard_map(
        on_device, mesh=mesh, in_specs=(whole, rows, rows, rows, P(), P(), P(), whole),
        out_specs=(whole, whole, P(("dp", "bricks"))), check_vma=False,
    )
```

```python
import functools

import jax
import jax.numpy as jnp
from jax import lax
from jax.experimental import pallas as pl
from jax.experimental.pallas import tpu as pltpu
from jax.sharding import PartitionSpec as P

MESH = pl.DeviceIdType.MESH
F32 = jnp.float32
BF16 = jnp.bfloat16
EPSILON = 1e-05
BIG = 1e30
LIMIT = 1e29
LAYERS = 64
ROWS = 3456
CUTS = (0, 4, 8, 11, 14)


def moved(index, stride, size, step):
    digit = (index // stride) % size
    return index + ((digit + step) % size - digit) * stride


def block_sum(v):
    return jnp.sum(v.reshape(v.shape[0] // 8, 8, v.shape[1]), axis=0)


def column_sum(v):
    return jnp.sum(v, axis=0, keepdims=True)


def packet(*rows):
    place = lax.broadcasted_iota(jnp.int32, (8, 256), 0)
    out = jnp.zeros((8, 256), F32)
    for i, row in enumerate(rows):
        out = jnp.where(place == i, row, out)
    return out


def pooled(parts):
    count = sum(p[2:3] for p in parts)
    first = sum(p[0:1] for p in parts)
    mean = first / jnp.maximum(count, 1.0)
    second = sum(p[1:2] for p in parts)
    for p in parts:
        apart = p[0:1] / jnp.maximum(p[2:3], 1.0) - mean
        second = second + p[2:3] * apart * apart
    return packet(first, second, count)


def group_sum(row):
    v = jnp.broadcast_to(row, (8, 256))
    lane = lax.broadcasted_iota(jnp.int32, (8, 256), 1)
    for step in (1, 2, 4):
        up = pltpu.roll(v, 256 - step, 1)
        down = pltpu.roll(v, step, 1)
        v = v + jnp.where((lane & step) == 0, up, down)
    return v[0:1]


def kernel(
    feat_hbm, cot_hbm, act, nbr, cond, gamma_in, beta_in, w_hbm,
    out, fgrad, wgrad,
    feat, cot, fs, zs, face_f, face_z, conds, conds_e, nbv, nbs,
    w_fwd, w_back, hz, zz, zt, wg, part, r1, r2, r3, zr,
    acc_f, acc_b, sg_s, outs, grads,
    own, got1, got2, back1, back2,
    w_sem, nb_sem, core_s, core_r, edge_s, edge_r, st_s, st_r, rs1_s, rs1_r, rs2_s, rs2_r, rs3_s, rs3_r, z_s, z_r,
    res_s, res_r, in_sem, out_sem,
):
    d = lax.axis_index("dp")
    b = lax.axis_index("bricks")
    c = b % 2
    layer = b // 2
    xm = (b // 8) % 4
    ym = (b // 2) % 4
    hm = b // 32
    other = b + 1 - 2 * c
    after0 = ((layer + 1) % LAYERS) * 2
    before1 = ((layer + LAYERS - 1) % LAYERS) * 2 + 1
    beside = jnp.where(c == 0, (layer + LAYERS - 1) % LAYERS, (layer + 1) % LAYERS) * 2

    def copy(src, dst, ssem, rsem, dev):
        return pltpu.make_async_remote_copy(
            src_ref=src, dst_ref=dst, send_sem=ssem, recv_sem=rsem, device_id=dev, device_id_type=MESH
        )

    in_copies = []
    for s in range(2):
        for k, (src, dst) in enumerate(((feat_hbm, feat), (cot_hbm, cot))):
            cp = pltpu.make_async_copy(src.at[s], dst.at[s], in_sem.at[s, k])
            cp.start()
            in_copies.append(cp)
    w_copy = pltpu.make_async_copy(w_hbm, w_fwd, w_sem)
    w_copy.start()

    barrier = pltpu.get_barrier_semaphore()
    partners = [{"bricks": moved(b, 1, 8, j)} for j in range(1, 8)]
    across = [moved(moved(b, 8, 4, j), 32, 4, i) for j in range(4) for i in range(4)][1:]
    partners += [{"bricks": dev} for dev in across[3:]]
    for j in range(4):
        up = moved(b, 32, 4, j)
        flip = up + 1 - 2 * c
        partners += [{"dp": 1 - d, "bricks": up}, {"dp": 1 - d, "bricks": flip}]
        if j:
            partners += [{"bricks": up}, {"bricks": flip}]
    partners += [{"bricks": after0}, {"bricks": before1}, {"bricks": beside}, {"bricks": beside + 1}]
    for dev in partners:
        pl.semaphore_signal(barrier, inc=1, device_id=dev, device_id_type=MESH)

    rows = [act[s : s + 1, 128 * j : 128 * j + 128] for s in range(2) for j in range(4)]
    flags = jnp.concatenate(rows, axis=0).astype(F32)
    count = jnp.sum(jnp.sum(flags, axis=1, keepdims=True), axis=0, keepdims=True)
    flags_t = flags.T
    first = jnp.zeros((8, 256), F32)
    for s in range(2):
        in_copies[2 * s].wait()
        in_copies[2 * s + 1].wait()
        for j in range(4):
            at = pl.ds(128 * j, 128)
            m = jnp.broadcast_to(flags_t[:, 4 * s + j : 4 * s + j + 1], (128, 256)) > 0.5
            f = feat[s, at, :].astype(F32)
            z = cot[s, at, :].astype(F32)
            fs[2 * c + s, at, :] = jnp.where(m, f, BIG).astype(BF16)
            zs[2 * c + s, at, :] = jnp.where(m, z, 0.0).astype(BF16)
            first = first + block_sum(jnp.where(m, f, 0.0))
    first = column_sum(first)
    local_mean = first / jnp.maximum(count, 1.0)
    second = jnp.zeros((8, 256), F32)
    for s in range(2):
        for j in range(4):
            f = fs[2 * c + s, pl.ds(128 * j, 128), :].astype(F32)
            apart = jnp.where(f < LIMIT, f - local_mean, 0.0)
            second = second + block_sum(apart * apart)
    second = column_sum(second)
    own[0] = packet(first, second, jnp.broadcast_to(count, (1, 256)))
    nbv[c] = jnp.zeros((8, 128), jnp.int32)
    nbv[c, 0:2, 0:27] = nbr[...]
    for s in range(2):
        conds[2 * c + s] = jnp.broadcast_to(cond[s : s + 1, :].astype(F32), (8, 256))
    pl.semaphore_wait(barrier, len(partners))

    def spread_start(stage, devices, boxes, base):
        sent = []
        for j, dev in enumerate(devices):
            cp = copy(own.at[stage], boxes.at[j], st_s.at[base + j], st_r.at[base + j], {"bricks": dev})
            cp.start()
            sent.append(cp)
        return sent

    def spread_end(sent, stage, boxes):
        for cp in sent:
            cp.wait()
        return [own[stage]] + [boxes[j] for j in range(len(sent))]

    near = [moved(b, 1, 8, j) for j in range(1, 8)]
    sent = spread_start(0, near, got1, 0)

    mine = pl.ds(2 * c, 2)
    core_copies = [
        copy(r.at[i], r.at[i], core_s.at[k], core_r.at[k], {"bricks": other})
        for k, (r, i) in enumerate(((nbv, c), (zs, mine), (fs, mine), (conds, mine)))
    ]
    for cp in core_copies:
        cp.start()
    edge_copies = []
    for k, (src, dst, up, down) in enumerate((
        (zs, face_z, pl.ds(448, 64), pl.ds(0, 64)),
        (fs, face_f, pl.ds(448, 64), pl.ds(0, 64)),
        (conds, conds_e, pl.ds(0, 8), pl.ds(0, 8)),
    )):
        for way, (at, dev) in enumerate(((up, after0), (down, before1))):
            cp = copy(
                src.at[mine, at], dst.at[mine], edge_s.at[2 * k + way], edge_r.at[k, c], {"bricks": dev}
            )
            cp.start()
            edge_copies.append(cp)

    def edge_wait(k, dst):
        for core in range(2):
            got = dst.at[pl.ds(2 * core, 2)]
            copy(got, got, edge_s.at[2 * k], edge_r.at[k, core], {"bricks": other}).wait_recv()

    for grid in (hz, zz):
        grid[:, 0:16, :] = jnp.zeros((10, 16, 768), BF16)
        grid[:, 272:288, :] = jnp.zeros((10, 16, 768), BF16)
    fs[4] = jnp.full((512, 256), BIG, BF16)
    zs[4] = jnp.zeros((512, 256), BF16)
    face_f[4] = jnp.full((64, 256), BIG, BF16)
    face_z[4] = jnp.zeros((64, 256), BF16)
    conds[4] = jnp.zeros((8, 256), F32)
    conds_e[4] = jnp.zeros((8, 256), F32)
    wg[pl.ds(128 + ROWS, 128), :] = jnp.zeros((128, 256), F32)

    w_copy.wait()

    def turn(g, carry):
        for e in range(3):
            w_back[g, pl.ds(256 * e, 256), :] = w_fwd[8 - g, pl.ds(256 * (2 - e), 256), :].T
        return carry

    lax.fori_loop(0, 9, turn, 0)

    merged = pooled(spread_end(sent, 0, got1))
    own[1] = merged
    sent = spread_start(1, across, got2, 7)

    core_copies[0].wait()
    nb_copy = pltpu.make_async_copy(nbv, nbs, nb_sem)
    nb_copy.start()
    nb_copy.wait()
    cy, cz, src, src_e = [], [], [], []
    here = []
    for j in range(4):
        def entry(k):
            return nbs[j // 2, j % 2, k]

        low_y = functools.reduce(jnp.maximum, [entry(9 * a + e) for a in range(3) for e in range(3)])
        low_z = functools.reduce(jnp.maximum, [entry(9 * a + 3 * e) for a in range(3) for e in range(3)])
        cy.append(jnp.where(low_y >= 0, 1, 0))
        cz.append(jnp.where(low_z >= 0, 1, 0))
        here.append(entry(13) >= 0)
    for q in range(4):
        qy, qz = q // 2, q % 2
        at, at_e = jnp.int32(4), jnp.int32(4)
        for j in range(4):
            at = jnp.where(here[j] & (cy[j] == qy) & (cz[j] == qz), j, at)
            t = nbs[j // 2, j % 2, 18 * c + 3 * (qy + 1 - cy[j]) + (qz + 1 - cz[j])]
            at_e = jnp.where(t >= 0, t & 3, at_e)
        src.append(at)
        src_e.append(at_e)

    zi = lax.broadcasted_iota(jnp.int32, (128, 256), 0) & 15

    def joined(left, right):
        pair = [v.reshape(8, 8, 256) for v in (left, right)]
        return jnp.concatenate(pair, axis=1).reshape(128, 256)

    def lay(grid, plane, half, v):
        at = pl.ds(16 + 128 * half, 128)
        grid[plane, at, 0:256] = jnp.where(zi == 0, 0.0, pltpu.roll(v, 1, 0)).astype(BF16)
        grid[plane, at, 256:512] = v.astype(BF16)
        grid[plane, at, 512:768] = jnp.where(zi == 15, 0.0, pltpu.roll(v, 127, 0)).astype(BF16)

    edge_plane = 9 * c

    core_copies[1].wait()
    edge_wait(0, face_z)

    def lay_z(x, carry):
        for half in range(2):
            at = pl.ds(pl.multiple_of(64 * x, 64), 64)
            v = joined(*[zs[src[2 * half + e], at, :].astype(F32) for e in range(2)])
            lay(zz, x + 1, half, v)
            zt[:, pl.ds(pl.multiple_of(256 * x + 128 * half, 128), 128)] = v.T.astype(BF16)
        return carry

    lax.fori_loop(0, 8, lay_z, 0)
    for half in range(2):
        lay(zz, edge_plane, half, joined(*[face_z[src_e[2 * half + e]].astype(F32) for e in range(2)]))

    def conv(grid, taps, acc, low, high):
        def step(g, carry):
            at = pl.ds(pl.multiple_of((g % 3) * 16, 16), 256)
            lhs = grid[pl.ds(4 * c + g // 3, 4), at, :].reshape(1024, 768)
            acc[...] += jnp.dot(lhs, taps[g], preferred_element_type=F32).reshape(4, 2, 8, 2, 8, 256)
            return carry

        lax.fori_loop(low, high, step, 0)

    acc_f[...] = jnp.zeros(acc_f.shape, F32)
    acc_b[...] = jnp.zeros(acc_b.shape, F32)
    conv(zz, w_back, acc_b, 0, 9)

    merged = pooled(spread_end(sent, 1, got2))
    total = merged[2:3]
    first, second = merged[0:1], merged[1:2]
    total_g = 8.0 * total
    mean = group_sum(first) / total_g
    apart = first / total - mean
    var = group_sum(second + total * apart * apart) / total_g
    inv_std = lax.rsqrt(var + EPSILON)
    gamma = gamma_in[...]
    beta = beta_in[...]
    slope = inv_std * gamma

    for cp in core_copies[2:]:
        cp.wait()
    edge_wait(1, face_f)
    edge_wait(2, conds_e)

    def activation(raw, shift):
        f = raw.astype(F32)
        m = f < LIMIT
        f = jnp.where(m, f, 0.0)
        apart = f - mean
        pre = apart * slope + (beta + shift[0:1])
        sigma = 1.0 / (1.0 + jnp.exp(-pre))
        return m, f, apart, pre, sigma

    def hidden(raw, shift):
        m, _, _, pre, sigma = activation(raw, shift)
        return jnp.where(m, pre * sigma, 0.0)

    def lay_h(x, carry):
        for half in range(2):
            at = pl.ds(pl.multiple_of(64 * x, 64), 64)
            slots = [src[2 * half + e] for e in range(2)]
            lay(hz, x + 1, half, joined(*[hidden(fs[j, at, :], conds[j]) for j in slots]))
        return carry

    lax.fori_loop(0, 8, lay_h, 0)
    for half in range(2):
        slots = [src_e[2 * half + e] for e in range(2)]
        lay(hz, edge_plane, half, joined(*[hidden(face_f[j], conds_e[j]) for j in slots]))

    def taps(low, high):
        def step(i, carry):
            t = 13 * c + i
            at = pl.ds(pl.multiple_of((t // 3) % 3 * 16, 16), 256)
            lanes = pl.ds(pl.multiple_of(t % 3 * 256, 256), 256)
            rhs = hz[pl.ds(t // 9, 8), at, lanes].reshape(2048, 256)
            made = jnp.dot(zt[...], rhs, preferred_element_type=F32)
            wg[pl.ds(pl.multiple_of(128 * (1 - c) + 256 * i, 128), 256), :] = made.T
            return carry

        lax.fori_loop(low, high, step, 0)

    way = ((8, 2), (2, 8))
    place = ((xm, ym), (ym, xm))

    def deal(h):
        def step(x, carry):
            base = pl.multiple_of(128 + 864 * h + 216 * x, 8)
            for y in range(4):
                low = 54 * y // 8 * 8
                v = wg[pl.ds(base + low, 64), :][54 * y - low : 54 * y - low + 56]
                part[0, x, h, y] = v[:, 0:128]
                part[1, y, h, x] = v[:, 128:256]
            return carry

        lax.fori_loop(0, 4, step, 0)

    live = {}

    def first_start(h):
        for k in range(2):
            a = place[k][0]
            for e, step in ((0, 1), (1, 3)):
                cp = copy(
                    part.at[k, (a + 2) % 4, h, pl.ds(2 * e, 2)], r1.at[k, h, e],
                    rs1_s.at[k, h, e], rs1_r.at[k, h, e], {"bricks": moved(b, way[k][0], 4, step)},
                )
                cp.start()
                live[1, k, h, e] = cp

    def second_start(h):
        for k in range(2):
            a = place[k][0]
            for e, step in ((0, 1), (1, 3)):
                live[1, k, h, e].wait()
                to = (a + step) % 4
                part[k, to, h, pl.ds(2 * e, 2)] += r1[k, h, e]
                cp = copy(
                    part.at[k, to, h], r2.at[k, h, e], rs2_s.at[k, h, e], rs2_r.at[k, h, e],
                    {"bricks": moved(b, way[k][0], 4, step)},
                )
                cp.start()
                live[2, k, h, e] = cp

    def third_start(h):
        for k in range(2):
            a, at = place[k]
            for e in range(2):
                live[2, k, h, e].wait()
            part[k, a, h] += r2[k, h, 0] + r2[k, h, 1]
            for j in range(1, 4):
                cp = copy(
                    part.at[k, a, h, (at + j) % 4], r3.at[k, h, j - 1], rs3_s.at[k, h, j - 1], rs3_r.at[k, h, j - 1],
                    {"bricks": moved(b, way[k][1], 4, j)},
                )
                cp.start()
                live[3, k, h, j] = cp

    side = jnp.where(c == d, 0, 1)

    def window(core):
        return pl.ds(pl.multiple_of(24 * core, 8), 32)

    def to_self(h):
        return (c == d) & (hm == h)

    def z_copies(h):
        one, two = [], []
        for k in range(2):
            a, at = place[k]
            base = b % 32 + 32 * h
            for group, core, dev in ((one, 1 - c, base + 1 - 2 * c), (two, c, base)):
                group.append(copy(
                    part.at[k, a, h, at, window(core)], zr.at[side, hm, k],
                    z_s.at[h, len(group), k], z_r.at[side, hm, k], {"dp": c, "bricks": dev},
                ))
        return one, two

    def z_start(h):
        for k in range(2):
            a, at = place[k]
            for j in range(1, 4):
                live[3, k, h, j].wait()
            part[k, a, h, at] += r3[k, h, 0] + r3[k, h, 1] + r3[k, h, 2]
        one, two = z_copies(h)
        for cp in one:
            cp.start()

        @pl.when(jnp.logical_not(to_self(h)))
        def _():
            for cp in two:
                cp.start()

        @pl.when(to_self(h))
        def _():
            for k in range(2):
                a, at = place[k]
                zr[0, h, k] = part[k, a, h, at, window(c), :]

    def z_end():
        for h in range(4):
            one, two = z_copies(h)
            for cp in one:
                cp.wait_send()

            @pl.when(jnp.logical_not(to_self(h)))
            def _():
                for cp in two:
                    cp.wait_send()
                for k in range(2):
                    copy(zr.at[0, h, k], zr.at[0, h, k], z_s.at[h, 0, k], z_r.at[0, h, k], {"bricks": other}).wait_recv()

            for k in range(2):
                copy(zr.at[1, h, k], zr.at[1, h, k], z_s.at[h, 0, k], z_r.at[1, h, k], {"bricks": other}).wait_recv()
        for k in range(2):
            v = sum(zr[e, h, k] for e in range(2) for h in range(4))
            wgrad[pl.ds(k, 27, stride=2), :] = jnp.where(c == 0, v[0:27], v[3:30])

    for h in range(4):
        taps(CUTS[h], CUTS[h + 1])
        deal(h)
        first_start(h)
        if h >= 2:
            second_start(h - 2)

    def slot_block(j, plane):
        at = pl.ds(pl.multiple_of(256 * c + 64 * plane, 64), 64)
        return at, activation(fs[j, at, :], conds[j])

    def back_pass(plane, carry):
        one, two = carry
        for j in range(4):
            at, (m, f, apart, pre, sigma) = slot_block(j, plane)
            back = acc_b[plane, cy[j], :, cz[j]].reshape(64, 256)
            sg = jnp.where(m, gamma * back * sigma * (1.0 + pre * (1.0 - sigma)), 0.0)
            sg_s[j, plane] = sg
            one = one + block_sum(sg)
            two = two + block_sum(sg * (apart * inv_std))
        return one, two

    zero = jnp.zeros((8, 256), F32)
    one, two = lax.fori_loop(0, 4, back_pass, (zero, zero))
    own[2] = packet(column_sum(one), column_sum(two))
    sent = spread_start(2, near, back1, 22)
    second_start(2)
    conv(hz, w_fwd, acc_f, 0, 2)
    second_start(3)
    third_start(0)
    conv(hz, w_fwd, acc_f, 2, 4)
    own[3] = sum(spread_end(sent, 2, back1))
    sent = spread_start(3, across, back2, 29)
    third_start(1)
    conv(hz, w_fwd, acc_f, 4, 6)
    z_start(0)
    conv(hz, w_fwd, acc_f, 6, 9)
    third_start(2)

    def out_pass(plane, carry):
        for j in range(4):
            at = pl.ds(pl.multiple_of(256 * c + 64 * plane, 64), 64)
            f = fs[j, at, :].astype(F32)
            made = acc_f[plane, cy[j], :, cz[j]].reshape(64, 256)
            outs[j, at, :] = jnp.where(f < LIMIT, f + made, 0.0).astype(BF16)
        return carry

    lax.fori_loop(0, 4, out_pass, 0)
    theirs = pl.ds(2 - 2 * c, 2)
    half_rows = pl.ds(pl.multiple_of(256 * c, 256), 256)

    def hand_over(ref, k):
        piece = ref.at[theirs, half_rows]
        cp = copy(piece, piece, res_s.at[k], res_r.at[k], {"bricks": other})
        cp.start()
        return cp

    out_copy = hand_over(outs, 0)
    z_start(1)
    sums = sum(spread_end(sent, 3, back2))
    grad_mean = group_sum(sums[0:1]) / total_g
    cross_mean = group_sum(sums[1:2]) / total_g

    def grad_pass(plane, carry):
        for j in range(4):
            at = pl.ds(pl.multiple_of(256 * c + 64 * plane, 64), 64)
            f = fs[j, at, :].astype(F32)
            x_hat = (f - mean) * inv_std
            v = inv_std * (sg_s[j, plane] - grad_mean - x_hat * cross_mean) + zs[j, at, :].astype(F32)
            grads[j, at, :] = jnp.where(f < LIMIT, v, 0.0).astype(BF16)
        return carry

    lax.fori_loop(0, 4, grad_pass, 0)
    grad_copy = hand_over(grads, 1)
    third_start(3)
    out_copy.wait()
    stores = [pltpu.make_async_copy(outs.at[mine], out, out_sem.at[0])]
    stores[0].start()
    z_start(2)
    grad_copy.wait()
    stores.append(pltpu.make_async_copy(grads.at[mine], fgrad, out_sem.at[1]))
    stores[1].start()
    z_start(3)
    for cp in edge_copies:
        cp.wait_send()
    for cp in stores:
        cp.wait()
    z_end()


def hand_out(*refs):
    sources, targets, held, sem_in, sem_out = refs[:3], refs[3:6], refs[6:9], refs[9], refs[10]
    steps = []
    for i in range(3):
        rows = sources[i].shape[0]
        for k in range(1 if i == 2 else rows):
            at = pl.ds(0, rows) if i == 2 else pl.ds(k, 1)
            steps.append((
                pltpu.make_async_copy(sources[i].at[at], held[i].at[at], sem_in.at[i, k]),
                pltpu.make_async_copy(held[i].at[at], targets[i].at[at], sem_out.at[i, k]),
            ))
    for load, _ in steps:
        load.start()
    for load, store in steps:
        load.wait()
        store.start()
    for _, store in steps:
        store.wait()


def on_device(features, active, neighbours, cond, gamma, beta, weight, cotangent):
    vmem = pl.BlockSpec(memory_space=pltpu.VMEM)
    dma = pltpu.SemaphoreType.DMA
    scratch = [
        pltpu.VMEM((2, 512, 256), BF16),
        pltpu.VMEM((2, 512, 256), BF16),
        pltpu.VMEM((5, 512, 256), BF16),
        pltpu.VMEM((5, 512, 256), BF16),
        pltpu.VMEM((5, 64, 256), BF16),
        pltpu.VMEM((5, 64, 256), BF16),
        pltpu.VMEM((5, 8, 256), F32),
        pltpu.VMEM((5, 8, 256), F32),
        pltpu.VMEM((2, 8, 128), jnp.int32),
        pltpu.SMEM((2, 8, 128), jnp.int32),
        pltpu.VMEM((9, 768, 256), BF16),
        pltpu.VMEM((9, 768, 256), BF16),
        pltpu.VMEM((10, 288, 768), BF16),
        pltpu.VMEM((10, 288, 768), BF16),
        pltpu.VMEM((256, 2048), BF16),
        pltpu.VMEM((ROWS + 256, 256), F32),
        pltpu.VMEM((2, 4, 4, 4, 56, 128), F32),
        pltpu.VMEM((2, 4, 2, 2, 56, 128), F32),
        pltpu.VMEM((2, 4, 2, 4, 56, 128), F32),
        pltpu.VMEM((2, 4, 3, 56, 128), F32),
        pltpu.VMEM((2, 4, 2, 32, 128), F32),
        pltpu.VMEM((4, 2, 8, 2, 8, 256), F32),
        pltpu.VMEM((4, 2, 8, 2, 8, 256), F32),
        pltpu.VMEM((4, 4, 64, 256), F32),
        pltpu.VMEM((4, 512, 256), BF16),
        pltpu.VMEM((4, 512, 256), BF16),
        pltpu.VMEM((4, 8, 256), F32),
        pltpu.VMEM((7, 8, 256), F32),
        pltpu.VMEM((15, 8, 256), F32),
        pltpu.VMEM((7, 8, 256), F32),
        pltpu.VMEM((15, 8, 256), F32),
        dma, dma, dma((4,)), dma((4,)), dma((6,)), dma((3, 2)), dma((44,)), dma((44,)),
        dma((2, 4, 2)), dma((2, 4, 2)), dma((2, 4, 2)), dma((2, 4, 2)),
        dma((2, 4, 3)), dma((2, 4, 3)), dma((4, 2, 2)), dma((2, 4, 2)),
        dma((2,)), dma((2,)), dma((2, 2)), dma((2,)),
    ]
    shapes = (
        jax.ShapeDtypeStruct((2, 512, 256), BF16),
        jax.ShapeDtypeStruct((2, 512, 256), BF16),
        jax.ShapeDtypeStruct((54, 128), F32),
    )
    anywhere = pl.BlockSpec(memory_space=pl.ANY)
    made = pl.pallas_call(
        kernel,
        out_shape=shapes,
        in_specs=[anywhere] * 2 + [vmem] * 5 + [anywhere],
        out_specs=(anywhere, anywhere, vmem),
        scratch_shapes=scratch,
        compiler_params=pltpu.CompilerParams(
            collective_id=0, has_side_effects=True, vmem_limit_bytes=60 * 2**20
        ),
        name="layer",
    )(
        features[0], cotangent[0], active[0], neighbours[0], cond[0],
        gamma.reshape(1, 256), beta.reshape(1, 256), weight.reshape(9, 768, 256),
    )
    output, feature_grad, weight_grad = pl.pallas_call(
        hand_out, out_shape=shapes, in_specs=[anywhere] * 3, out_specs=(anywhere,) * 3,
        scratch_shapes=[pltpu.VMEM(v.shape, v.dtype) for v in shapes] + [dma((3, 2)), dma((3, 2))],
        compiler_params=pltpu.CompilerParams(vmem_limit_bytes=60 * 2**20), name="hand_out",
    )(*made)
    return output[None], feature_grad[None], weight_grad.reshape(-1)


def solution(mesh):
    whole = P("dp", "bricks", None, None)
    rows = P("dp", "bricks", None)
    return jax.shard_map(
        on_device, mesh=mesh, in_specs=(whole, rows, rows, rows, P(), P(), P(), whole),
        out_specs=(whole, whole, P(("dp", "bricks"))), check_vma=False,
    )
```

```python
import functools

import jax
import jax.numpy as jnp
from jax import lax
from jax.experimental import pallas as pl
from jax.experimental.pallas import tpu as pltpu
from jax.sharding import PartitionSpec as P

MESH = pl.DeviceIdType.MESH
F32 = jnp.float32
BF16 = jnp.bfloat16
EPSILON = 1e-05
BIG = 1e30
LIMIT = 1e29
LAYERS = 64
ROWS = 3456
CUTS = (0, 2, 3, 4, 5)
LEAD = 384


def moved(index, stride, size, step):
    digit = (index // stride) % size
    return index + ((digit + step) % size - digit) * stride


def block_sum(v):
    return jnp.sum(v.reshape(v.shape[0] // 8, 8, v.shape[1]), axis=0)


def column_sum(v):
    return jnp.sum(v, axis=0, keepdims=True)


def packet(*rows):
    place = lax.broadcasted_iota(jnp.int32, (8, 256), 0)
    out = jnp.zeros((8, 256), F32)
    for i, row in enumerate(rows):
        out = jnp.where(place == i, row, out)
    return out


def pooled(parts):
    count = sum(p[2:3] for p in parts)
    first = sum(p[0:1] for p in parts)
    mean = first / jnp.maximum(count, 1.0)
    second = sum(p[1:2] for p in parts)
    for p in parts:
        apart = p[0:1] / jnp.maximum(p[2:3], 1.0) - mean
        second = second + p[2:3] * apart * apart
    return packet(first, second, count)


def group_sum(row):
    v = jnp.broadcast_to(row, (8, 256))
    lane = lax.broadcasted_iota(jnp.int32, (8, 256), 1)
    for step in (1, 2, 4):
        up = pltpu.roll(v, 256 - step, 1)
        down = pltpu.roll(v, step, 1)
        v = v + jnp.where((lane & step) == 0, up, down)
    return v[0:1]


def kernel(
    feat_hbm, cot_hbm, act, nbr, cond, gamma_in, beta_in, w_hbm,
    out, fgrad, wgrad,
    feat, cot, fs, zs, face_f, face_z, conds, conds_e, nbv, nbs,
    w_fwd, w_back, hz, zz, wg, part, r1, r2, r3, zr,
    acc_f, acc_b, sg_s, outs, grads,
    own, got1, got2, back1, back2,
    w_sem, nb_sem, core_s, core_r, edge_s, edge_r, st_s, st_r, rs1_s, rs1_r, rs2_s, rs2_r, rs3_s, rs3_r, z_s, z_r,
    res_s, res_r, in_sem, out_sem,
):
    d = lax.axis_index("dp")
    b = lax.axis_index("bricks")
    c = b % 2
    layer = b // 2
    xm = (b // 8) % 4
    ym = (b // 2) % 4
    hm = b // 32
    after0 = ((layer + 1) % LAYERS) * 2
    before1 = ((layer + LAYERS - 1) % LAYERS) * 2 + 1
    beside = jnp.where(c == 0, (layer + LAYERS - 1) % LAYERS, (layer + 1) % LAYERS) * 2

    def copy(src, dst, ssem, rsem, dev):
        return pltpu.make_async_remote_copy(
            src_ref=src, dst_ref=dst, send_sem=ssem, recv_sem=rsem, device_id=dev, device_id_type=MESH
        )

    in_copies = []
    for k, (src, dst) in enumerate(((feat_hbm, feat), (cot_hbm, cot))):
        for s in range(2):
            cp = pltpu.make_async_copy(src.at[s], dst.at[s], in_sem.at[s, k])
            cp.start()
            in_copies.append(cp)
    w_copy = pltpu.make_async_copy(w_hbm, w_fwd, w_sem)

    barrier = pltpu.get_barrier_semaphore()
    other = b + 1 - 2 * c
    near = []
    for j in range(4):
        up = moved(b, 32, 4, j)
        near += [up, up + 1 - 2 * c]
    across = [moved(moved(b, 8, 4, j), 2, 4, i) for j in range(4) for i in range(4)]
    partners = [{"dp": 1 - d, "bricks": dev} for dev in near]
    partners += [{"bricks": dev} for dev in near[1:] + across[1:]]
    partners += [{"bricks": after0}, {"bricks": before1}, {"bricks": beside}, {"bricks": beside + 1}]
    for dev in partners:
        pl.semaphore_signal(barrier, inc=1, device_id=dev, device_id_type=MESH)

    rows = [act[s : s + 1, 128 * j : 128 * j + 128] for s in range(2) for j in range(4)]
    flags = jnp.concatenate(rows, axis=0).astype(F32)
    count = jnp.sum(jnp.sum(flags, axis=1, keepdims=True), axis=0, keepdims=True)
    flags_t = flags.T
    def active_rows(s, j):
        return jnp.broadcast_to(flags_t[:, 4 * s + j : 4 * s + j + 1], (128, 256)) > 0.5

    shift = None
    first = jnp.zeros((8, 256), F32)
    second = jnp.zeros((8, 256), F32)
    for s in range(2):
        in_copies[s].wait()
        for j in range(4):
            m = active_rows(s, j)
            f = feat[s, pl.ds(128 * j, 128), :].astype(F32)
            if shift is None:
                held = column_sum(block_sum(jnp.where(m, 1.0, 0.0)))
                shift = column_sum(block_sum(jnp.where(m, f, 0.0))) / jnp.maximum(held, 1.0)
            apart = jnp.where(m, f - shift, 0.0)
            first = first + block_sum(apart)
            second = second + block_sum(apart * apart)
    first = column_sum(first)
    second = column_sum(second) - first * first / jnp.maximum(count, 1.0)
    first = first + count * shift
    own[0] = packet(first, second, jnp.broadcast_to(count, (1, 256)))
    pl.semaphore_wait(barrier, len(partners))

    def spread_start(stage, devices, boxes, base):
        sent = []
        for j, dev in enumerate(devices):
            cp = copy(own.at[stage], boxes.at[j], st_s.at[base + j], st_r.at[base + j], {"bricks": dev})
            cp.start()
            sent.append(cp)
        return sent

    def spread_end(sent, stage, boxes):
        for cp in sent:
            cp.wait()
        return [own[stage]] + [boxes[j] for j in range(len(sent))]

    sent = spread_start(0, near[1:], got1, 0)

    in_copies[2].wait()
    in_copies[3].wait()
    w_copy.start()
    for s in range(2):
        for j in range(4):
            at = pl.ds(128 * j, 128)
            m = active_rows(s, j)
            fs[2 * c + s, at, :] = jnp.where(m, feat[s, at, :].astype(F32), BIG).astype(BF16)
            zs[2 * c + s, at, :] = jnp.where(m, cot[s, at, :].astype(F32), 0.0).astype(BF16)
    nbv[c] = jnp.zeros((8, 128), jnp.int32)
    nbv[c, 0:2, 0:27] = nbr[...]
    for s in range(2):
        conds[2 * c + s] = jnp.broadcast_to(cond[s : s + 1, :].astype(F32), (8, 256))
    mine = pl.ds(2 * c, 2)
    core_copies = [
        copy(r.at[i], r.at[i], core_s.at[k], core_r.at[k], {"bricks": other})
        for k, (r, i) in enumerate(((nbv, c), (zs, mine), (fs, mine), (conds, mine)))
    ]
    for cp in core_copies:
        cp.start()
    edge_copies = []
    for k, (src, dst, up, down) in enumerate((
        (zs, face_z, pl.ds(448, 64), pl.ds(0, 64)),
        (fs, face_f, pl.ds(448, 64), pl.ds(0, 64)),
        (conds, conds_e, pl.ds(0, 8), pl.ds(0, 8)),
    )):
        for way, (at, dev) in enumerate(((up, after0), (down, before1))):
            cp = copy(
                src.at[mine, at], dst.at[mine], edge_s.at[2 * k + way], edge_r.at[k, c], {"bricks": dev}
            )
            cp.start()
            edge_copies.append(cp)

    def edge_wait(k, dst):
        for core in range(2):
            got = dst.at[pl.ds(2 * core, 2)]
            copy(got, got, edge_s.at[2 * k], edge_r.at[k, core], {"bricks": other}).wait_recv()

    for grid in (hz, zz):
        grid[:, 0:16, :] = jnp.zeros((10, 16, 768), BF16)
        grid[:, 272:288, :] = jnp.zeros((10, 16, 768), BF16)
    fs[4] = jnp.full((512, 256), BIG, BF16)
    zs[4] = jnp.zeros((512, 256), BF16)
    face_f[4] = jnp.full((64, 256), BIG, BF16)
    face_z[4] = jnp.zeros((64, 256), BF16)
    conds[4] = jnp.zeros((8, 256), F32)
    conds_e[4] = jnp.zeros((8, 256), F32)
    wg[pl.ds(LEAD + ROWS, 8), :] = jnp.zeros((8, 256), F32)

    w_copy.wait()

    def turn(g, carry):
        for e in range(3):
            w_back[g, pl.ds(256 * e, 256), :] = w_fwd[8 - g, pl.ds(256 * (2 - e), 256), :].T
        return carry

    lax.fori_loop(0, 9, turn, 0)

    core_copies[0].wait()
    nb_copy = pltpu.make_async_copy(nbv, nbs, nb_sem)
    nb_copy.start()
    nb_copy.wait()
    cy, cz, src, src_e = [], [], [], []
    here = []
    for j in range(4):
        def entry(k):
            return nbs[j // 2, j % 2, k]

        low_y = functools.reduce(jnp.maximum, [entry(9 * a + e) for a in range(3) for e in range(3)])
        low_z = functools.reduce(jnp.maximum, [entry(9 * a + 3 * e) for a in range(3) for e in range(3)])
        cy.append(jnp.where(low_y >= 0, 1, 0))
        cz.append(jnp.where(low_z >= 0, 1, 0))
        here.append(entry(13) >= 0)
    for q in range(4):
        qy, qz = q // 2, q % 2
        at, at_e = jnp.int32(4), jnp.int32(4)
        for j in range(4):
            at = jnp.where(here[j] & (cy[j] == qy) & (cz[j] == qz), j, at)
            t = nbs[j // 2, j % 2, 18 * c + 3 * (qy + 1 - cy[j]) + (qz + 1 - cz[j])]
            at_e = jnp.where(t >= 0, t & 3, at_e)
        src.append(at)
        src_e.append(at_e)

    zi = lax.broadcasted_iota(jnp.int32, (128, 256), 0) & 15

    def joined(left, right):
        pair = [v.reshape(8, 8, 256) for v in (left, right)]
        return jnp.concatenate(pair, axis=1).reshape(128, 256)

    def lay(grid, plane, half, v):
        at = pl.ds(16 + 128 * half, 128)
        grid[plane, at, 0:256] = jnp.where(zi == 0, 0.0, pltpu.roll(v, 1, 0)).astype(BF16)
        grid[plane, at, 256:512] = v.astype(BF16)
        grid[plane, at, 512:768] = jnp.where(zi == 15, 0.0, pltpu.roll(v, 127, 0)).astype(BF16)

    edge_plane = 9 * c

    core_copies[1].wait()

    def lay_z(x, carry):
        for half in range(2):
            at = pl.ds(pl.multiple_of(64 * x, 64), 64)
            v = joined(*[zs[src[2 * half + e], at, :].astype(F32) for e in range(2)])
            lay(zz, x + 1, half, v)
        return carry

    lax.fori_loop(0, 8, lay_z, 0)

    merged = pooled(spread_end(sent, 0, got1))
    own[1] = merged
    sent = spread_start(1, across[1:], got2, 7)

    def conv(grid, taps, acc, kx):
        planes = pl.ds(4 * c + kx, 4)
        lhs = jnp.concatenate([grid[planes, 16 * e : 16 * e + 256, :].reshape(1024, 768) for e in range(3)], axis=1)
        rhs = taps[3 * kx : 3 * kx + 3].reshape(2304, 256)
        made = jnp.dot(lhs, rhs, preferred_element_type=F32).reshape(4, 2, 8, 2, 8, 256)
        acc[...] = made if kx == 1 else acc[...] + made

    conv(zz, w_back, acc_b, 1)
    edge_wait(0, face_z)
    for half in range(2):
        lay(zz, edge_plane, half, joined(*[face_z[src_e[2 * half + e]].astype(F32) for e in range(2)]))
    conv(zz, w_back, acc_b, 0)
    conv(zz, w_back, acc_b, 2)

    merged = pooled(spread_end(sent, 1, got2))
    total = merged[2:3]
    first, second = merged[0:1], merged[1:2]
    total_g = 8.0 * total
    mean = group_sum(first) / total_g
    apart = first / total - mean
    var = group_sum(second + total * apart * apart) / total_g
    inv_std = lax.rsqrt(var + EPSILON)
    gamma = gamma_in[...]
    beta = beta_in[...]
    slope = inv_std * gamma

    for cp in core_copies[2:]:
        cp.wait()
    edge_wait(1, face_f)
    edge_wait(2, conds_e)

    def activation(raw, shift):
        f = raw.astype(F32)
        m = f < LIMIT
        f = jnp.where(m, f, 0.0)
        apart = f - mean
        pre = apart * slope + (beta + shift[0:1])
        sigma = 1.0 / (1.0 + jnp.exp(-pre))
        return m, f, apart, pre, sigma

    def hidden(raw, shift):
        m, _, _, pre, sigma = activation(raw, shift)
        return jnp.where(m, pre * sigma, 0.0)

    def lay_h(x, carry):
        for half in range(2):
            at = pl.ds(pl.multiple_of(64 * x, 64), 64)
            slots = [src[2 * half + e] for e in range(2)]
            lay(hz, x + 1, half, joined(*[hidden(fs[j, at, :], conds[j]) for j in slots]))
        return carry

    lax.fori_loop(0, 8, lay_h, 0)
    for half in range(2):
        slots = [src_e[2 * half + e] for e in range(2)]
        lay(hz, edge_plane, half, joined(*[hidden(face_f[j], conds_e[j]) for j in slots]))

    def taps(low, high):
        def step(i, carry):
            g = 4 * c + i
            at = pl.ds(pl.multiple_of(g % 3 * 16, 16), 256)
            lhs = hz[pl.ds(g // 3, 8), at, :].reshape(2048, 768)
            center = zz[1:9, 16:272, 256:512].reshape(2048, 256)
            wg[pl.ds(pl.multiple_of(LEAD * (1 - c) + 768 * i, 128), 768), :] = lax.dot_general(
                lhs, center, (((0,), (0,)), ((), ())), preferred_element_type=F32
            )
            return carry

        lax.fori_loop(low, high, step, 0)

    way = ((8, 2), (2, 8))
    place = ((xm, ym), (ym, xm))

    def deal(h):
        def step(x, carry):
            base = pl.multiple_of(LEAD + 864 * h + 216 * x, 8)
            for y in range(4):
                low = 54 * y // 8 * 8
                v = wg[pl.ds(base + low, 64), :][54 * y - low : 54 * y - low + 56]
                part[0, x, h, y] = v[:, 0:128]
                part[1, y, h, x] = v[:, 128:256]
            return carry

        lax.fori_loop(0, 4, step, 0)

    live = {}

    def first_start(h):
        for k in range(2):
            a = place[k][0]
            for e, step in ((0, 1), (1, 3)):
                cp = copy(
                    part.at[k, (a + 2) % 4, h, pl.ds(2 * e, 2)], r1.at[k, h, e],
                    rs1_s.at[k, h, e], rs1_r.at[k, h, e], {"bricks": moved(b, way[k][0], 4, step)},
                )
                cp.start()
                live[1, k, h, e] = cp

    def second_start(h):
        for k in range(2):
            a = place[k][0]
            for e, step in ((0, 1), (1, 3)):
                live[1, k, h, e].wait()
                to = (a + step) % 4
                part[k, to, h, pl.ds(2 * e, 2)] += r1[k, h, e]
                cp = copy(
                    part.at[k, to, h], r2.at[k, h, e], rs2_s.at[k, h, e], rs2_r.at[k, h, e],
                    {"bricks": moved(b, way[k][0], 4, step)},
                )
                cp.start()
                live[2, k, h, e] = cp

    def third_start(h):
        for k in range(2):
            a, at = place[k]
            for e in range(2):
                live[2, k, h, e].wait()
            part[k, a, h] += r2[k, h, 0] + r2[k, h, 1]
            for j in range(1, 4):
                cp = copy(
                    part.at[k, a, h, (at + j) % 4], r3.at[k, h, j - 1], rs3_s.at[k, h, j - 1], rs3_r.at[k, h, j - 1],
                    {"bricks": moved(b, way[k][1], 4, j)},
                )
                cp.start()
                live[3, k, h, j] = cp

    side = jnp.where(c == d, 0, 1)

    def window(core):
        return pl.ds(pl.multiple_of(24 * core, 8), 32)

    def to_self(h):
        return (c == d) & (hm == h)

    def z_copies(h):
        one, two = [], []
        for k in range(2):
            a, at = place[k]
            base = b % 32 + 32 * h
            for group, core, dev in ((one, 1 - c, base + 1 - 2 * c), (two, c, base)):
                group.append(copy(
                    part.at[k, a, h, at, window(core)], zr.at[side, hm, k],
                    z_s.at[h, len(group), k], z_r.at[side, hm, k], {"dp": c, "bricks": dev},
                ))
        return one, two

    def z_start(h):
        for k in range(2):
            a, at = place[k]
            for j in range(1, 4):
                live[3, k, h, j].wait()
            part[k, a, h, at] += r3[k, h, 0] + r3[k, h, 1] + r3[k, h, 2]
        one, two = z_copies(h)
        for cp in one:
            cp.start()

        @pl.when(jnp.logical_not(to_self(h)))
        def _():
            for cp in two:
                cp.start()

        @pl.when(to_self(h))
        def _():
            for k in range(2):
                a, at = place[k]
                zr[0, h, k] = part[k, a, h, at, window(c), :]

    def z_end():
        for h in range(4):
            one, two = z_copies(h)
            for cp in one:
                cp.wait_send()

            @pl.when(jnp.logical_not(to_self(h)))
            def _():
                for cp in two:
                    cp.wait_send()
                for k in range(2):
                    copy(zr.at[0, h, k], zr.at[0, h, k], z_s.at[h, 0, k], z_r.at[0, h, k], {"bricks": other}).wait_recv()

            for k in range(2):
                copy(zr.at[1, h, k], zr.at[1, h, k], z_s.at[h, 0, k], z_r.at[1, h, k], {"bricks": other}).wait_recv()
        for k in range(2):
            v = sum(zr[e, h, k] for e in range(2) for h in range(4))
            wgrad[pl.ds(k, 27, stride=2), :] = jnp.where(c == 0, v[0:27], v[3:30])

    def slot_block(j, plane):
        at = pl.ds(pl.multiple_of(256 * c + 64 * plane, 64), 64)
        return at, activation(fs[j, at, :], conds[j])

    def back_pass(plane, carry):
        one, two = carry
        for j in range(4):
            at, (m, f, apart, pre, sigma) = slot_block(j, plane)
            back = acc_b[plane, cy[j], :, cz[j]].reshape(64, 256)
            sg = jnp.where(m, gamma * back * sigma * (1.0 + pre * (1.0 - sigma)), 0.0)
            sg_s[j, plane] = sg
            one = one + block_sum(sg)
            two = two + block_sum(sg * (apart * inv_std))
        return one, two

    def back_start():
        zero = jnp.zeros((8, 256), F32)
        one, two = lax.fori_loop(0, 4, back_pass, (zero, zero))
        own[2] = packet(column_sum(one), column_sum(two))
        return spread_start(2, across[1:], back1, 22)

    def out_pass(plane, carry):
        for j in range(4):
            at = pl.ds(pl.multiple_of(256 * c + 64 * plane, 64), 64)
            f = fs[j, at, :].astype(F32)
            made = acc_f[plane, cy[j], :, cz[j]].reshape(64, 256)
            outs[j, at, :] = jnp.where(f < LIMIT, f + made, 0.0).astype(BF16)
        return carry

    theirs = pl.ds(2 - 2 * c, 2)
    half_rows = pl.ds(pl.multiple_of(256 * c, 256), 256)

    def hand_over(ref, k):
        piece = ref.at[theirs, half_rows]
        cp = copy(piece, piece, res_s.at[k], res_r.at[k], {"bricks": other})
        cp.start()
        return cp

    def grad_pass(grad_mean, cross_mean, plane, carry):
        for j in range(4):
            at = pl.ds(pl.multiple_of(256 * c + 64 * plane, 64), 64)
            f = fs[j, at, :].astype(F32)
            x_hat = (f - mean) * inv_std
            v = inv_std * (sg_s[j, plane] - grad_mean - x_hat * cross_mean) + zs[j, at, :].astype(F32)
            grads[j, at, :] = jnp.where(f < LIMIT, v, 0.0).astype(BF16)
        return carry

    for h in range(4):
        taps(CUTS[h], CUTS[h + 1])
        deal(h)
        first_start(h)
        if h == 0:
            sent = back_start()
        if h >= 1:
            second_start(h - 1)
    own[3] = sum(spread_end(sent, 2, back1))
    sent = spread_start(3, near[1:], back2, 37)
    conv(hz, w_fwd, acc_f, 1)
    second_start(3)
    third_start(0)
    conv(hz, w_fwd, acc_f, 0)
    third_start(1)
    sums = sum(spread_end(sent, 3, back2))
    grad_mean = group_sum(sums[0:1]) / total_g
    cross_mean = group_sum(sums[1:2]) / total_g
    lax.fori_loop(0, 4, functools.partial(grad_pass, grad_mean, cross_mean), 0)
    grad_copy = hand_over(grads, 1)
    third_start(2)
    conv(hz, w_fwd, acc_f, 2)
    lax.fori_loop(0, 4, out_pass, 0)
    out_copy = hand_over(outs, 0)
    third_start(3)
    z_start(0)
    z_start(1)
    z_start(2)
    stores = []
    for k, (cp, ref, to) in enumerate(((out_copy, outs, out), (grad_copy, grads, fgrad))):
        cp.wait()
        stores.append(pltpu.make_async_copy(ref.at[mine], to, out_sem.at[k]))
        stores[k].start()
    z_start(3)
    for cp in edge_copies:
        cp.wait_send()
    for cp in stores:
        cp.wait()
    z_end()


def hand_out(*refs):
    sources, targets, held, sem_in, sem_out = refs[:3], refs[3:6], refs[6:9], refs[9], refs[10]
    steps = []
    for i in range(3):
        rows = sources[i].shape[0]
        for k in range(1 if i == 2 else rows):
            at = pl.ds(0, rows) if i == 2 else pl.ds(k, 1)
            steps.append((
                pltpu.make_async_copy(sources[i].at[at], held[i].at[at], sem_in.at[i, k]),
                pltpu.make_async_copy(held[i].at[at], targets[i].at[at], sem_out.at[i, k]),
            ))
    for load, _ in steps:
        load.start()
    for load, store in steps:
        load.wait()
        store.start()
    for _, store in steps:
        store.wait()


def on_device(features, active, neighbours, cond, gamma, beta, weight, cotangent):
    vmem = pl.BlockSpec(memory_space=pltpu.VMEM)
    dma = pltpu.SemaphoreType.DMA
    scratch = [
        pltpu.VMEM((2, 512, 256), BF16),
        pltpu.VMEM((2, 512, 256), BF16),
        pltpu.VMEM((5, 512, 256), BF16),
        pltpu.VMEM((5, 512, 256), BF16),
        pltpu.VMEM((5, 64, 256), BF16),
        pltpu.VMEM((5, 64, 256), BF16),
        pltpu.VMEM((5, 8, 256), F32),
        pltpu.VMEM((5, 8, 256), F32),
        pltpu.VMEM((2, 8, 128), jnp.int32),
        pltpu.SMEM((2, 8, 128), jnp.int32),
        pltpu.VMEM((9, 768, 256), BF16),
        pltpu.VMEM((9, 768, 256), BF16),
        pltpu.VMEM((10, 288, 768), BF16),
        pltpu.VMEM((10, 288, 768), BF16),
        pltpu.VMEM((LEAD + 3840, 256), F32),
        pltpu.VMEM((2, 4, 4, 4, 56, 128), F32),
        pltpu.VMEM((2, 4, 2, 2, 56, 128), F32),
        pltpu.VMEM((2, 4, 2, 4, 56, 128), F32),
        pltpu.VMEM((2, 4, 3, 56, 128), F32),
        pltpu.VMEM((2, 4, 2, 32, 128), F32),
        pltpu.VMEM((4, 2, 8, 2, 8, 256), F32),
        pltpu.VMEM((4, 2, 8, 2, 8, 256), F32),
        pltpu.VMEM((4, 4, 64, 256), F32),
        pltpu.VMEM((4, 512, 256), BF16),
        pltpu.VMEM((4, 512, 256), BF16),
        pltpu.VMEM((4, 8, 256), F32),
        pltpu.VMEM((7, 8, 256), F32),
        pltpu.VMEM((15, 8, 256), F32),
        pltpu.VMEM((15, 8, 256), F32),
        pltpu.VMEM((7, 8, 256), F32),
        dma, dma, dma((4,)), dma((4,)), dma((6,)), dma((3, 2)), dma((44,)), dma((44,)),
        dma((2, 4, 2)), dma((2, 4, 2)), dma((2, 4, 2)), dma((2, 4, 2)),
        dma((2, 4, 3)), dma((2, 4, 3)), dma((4, 2, 2)), dma((2, 4, 2)),
        dma((2,)), dma((2,)), dma((2, 2)), dma((2,)),
    ]
    shapes = (
        jax.ShapeDtypeStruct((2, 512, 256), BF16),
        jax.ShapeDtypeStruct((2, 512, 256), BF16),
        jax.ShapeDtypeStruct((54, 128), F32),
    )
    anywhere = pl.BlockSpec(memory_space=pl.ANY)
    made = pl.pallas_call(
        kernel,
        out_shape=shapes,
        in_specs=[anywhere] * 2 + [vmem] * 5 + [anywhere],
        out_specs=(anywhere, anywhere, vmem),
        scratch_shapes=scratch,
        compiler_params=pltpu.CompilerParams(
            collective_id=0, has_side_effects=True, vmem_limit_bytes=60 * 2**20
        ),
        name="layer",
    )(
        features[0], cotangent[0], active[0], neighbours[0], cond[0],
        gamma.reshape(1, 256), beta.reshape(1, 256), weight.reshape(9, 768, 256),
    )
    output, feature_grad, weight_grad = pl.pallas_call(
        hand_out, out_shape=shapes, in_specs=[anywhere] * 3, out_specs=(anywhere,) * 3,
        scratch_shapes=[pltpu.VMEM(v.shape, v.dtype) for v in shapes] + [dma((3, 2)), dma((3, 2))],
        compiler_params=pltpu.CompilerParams(vmem_limit_bytes=60 * 2**20), name="hand_out",
    )(*made)
    return output[None], feature_grad[None], weight_grad.reshape(-1)


def solution(mesh):
    whole = P("dp", "bricks", None, None)
    rows = P("dp", "bricks", None)
    return jax.shard_map(
        on_device, mesh=mesh, in_specs=(whole, rows, rows, rows, P(), P(), P(), whole),
        out_specs=(whole, whole, P(("dp", "bricks"))), check_vma=False,
    )
```

```python
import functools

import jax
import jax.numpy as jnp
from jax import lax
from jax.experimental import pallas as pl
from jax.experimental.pallas import tpu as pltpu
from jax.sharding import PartitionSpec as P

MESH = pl.DeviceIdType.MESH
F32 = jnp.float32
BF16 = jnp.bfloat16
EPSILON = 1e-05
BIG = 1e30
LIMIT = 1e29
LAYERS = 64
ROWS = 3456
CUTS = (0, 2, 3, 4, 5)
LEAD = 384


def moved(index, stride, size, step):
    digit = (index // stride) % size
    return index + ((digit + step) % size - digit) * stride


def block_sum(v):
    return jnp.sum(v.reshape(v.shape[0] // 8, 8, v.shape[1]), axis=0)


def column_sum(v):
    return jnp.sum(v, axis=0, keepdims=True)


def packet(*rows):
    place = lax.broadcasted_iota(jnp.int32, (8, 256), 0)
    out = jnp.zeros((8, 256), F32)
    for i, row in enumerate(rows):
        out = jnp.where(place == i, row, out)
    return out


def pooled(parts):
    count = sum(p[2:3] for p in parts)
    first = sum(p[0:1] for p in parts)
    mean = first / jnp.maximum(count, 1.0)
    second = sum(p[1:2] for p in parts)
    for p in parts:
        apart = p[0:1] / jnp.maximum(p[2:3], 1.0) - mean
        second = second + p[2:3] * apart * apart
    return packet(first, second, count)


def group_sum(row):
    v = jnp.broadcast_to(row, (8, 256))
    lane = lax.broadcasted_iota(jnp.int32, (8, 256), 1)
    for step in (1, 2, 4):
        up = pltpu.roll(v, 256 - step, 1)
        down = pltpu.roll(v, step, 1)
        v = v + jnp.where((lane & step) == 0, up, down)
    return v[0:1]


def kernel(
    feat_hbm, cot_hbm, act, nbr, cond, gamma_in, beta_in, w_hbm,
    out, fgrad, wgrad,
    feat, cot, fs, zs, face_f, face_z, conds, conds_e, nbv, nbs,
    w_fwd, w_back, hz, zz, wg, part, r1, r2, r3, zr,
    acc_f, acc_b, sg_s, outs, grads,
    own, got1, got2, back1, back2,
    w_sem, nb_sem, core_s, core_r, edge_s, edge_r, st_s, st_r, rs1_s, rs1_r, rs2_s, rs2_r, rs3_s, rs3_r, z_s, z_r,
    res_s, res_r, in_sem, out_sem,
):
    d = lax.axis_index("dp")
    b = lax.axis_index("bricks")
    c = b % 2
    layer = b // 2
    xm = (b // 8) % 4
    ym = (b // 2) % 4
    hm = b // 32
    after0 = ((layer + 1) % LAYERS) * 2
    before1 = ((layer + LAYERS - 1) % LAYERS) * 2 + 1
    beside = jnp.where(c == 0, (layer + LAYERS - 1) % LAYERS, (layer + 1) % LAYERS) * 2

    def copy(src, dst, ssem, rsem, dev):
        return pltpu.make_async_remote_copy(
            src_ref=src, dst_ref=dst, send_sem=ssem, recv_sem=rsem, device_id=dev, device_id_type=MESH
        )

    in_copies = []
    for k, (src, dst) in enumerate(((feat_hbm, feat), (cot_hbm, cot))):
        for s in range(2):
            cp = pltpu.make_async_copy(src.at[s], dst.at[s], in_sem.at[s, k])
            cp.start()
            in_copies.append(cp)
    w_copy = pltpu.make_async_copy(w_hbm, w_fwd, w_sem)

    barrier = pltpu.get_barrier_semaphore()
    other = b + 1 - 2 * c
    near = []
    for j in range(4):
        up = moved(b, 32, 4, j)
        near += [up, up + 1 - 2 * c]
    across = [moved(moved(b, 8, 4, j), 2, 4, i) for j in range(4) for i in range(4)]
    partners = [{"dp": 1 - d, "bricks": dev} for dev in near]
    partners += [{"bricks": dev} for dev in near[1:] + across[1:]]
    partners += [{"bricks": after0}, {"bricks": before1}, {"bricks": beside}, {"bricks": beside + 1}]
    for dev in partners:
        pl.semaphore_signal(barrier, inc=1, device_id=dev, device_id_type=MESH)

    rows = [act[s : s + 1, 128 * j : 128 * j + 128] for s in range(2) for j in range(4)]
    flags = jnp.concatenate(rows, axis=0).astype(F32)
    count = jnp.sum(jnp.sum(flags, axis=1, keepdims=True), axis=0, keepdims=True)
    flags_t = flags.T
    def active_rows(s, j):
        return jnp.broadcast_to(flags_t[:, 4 * s + j : 4 * s + j + 1], (128, 256)) > 0.5

    shift = None
    first = jnp.zeros((8, 256), F32)
    second = jnp.zeros((8, 256), F32)
    for s in range(2):
        in_copies[s].wait()
        for j in range(4):
            m = active_rows(s, j)
            f = feat[s, pl.ds(128 * j, 128), :].astype(F32)
            if shift is None:
                held = column_sum(block_sum(jnp.where(m, 1.0, 0.0)))
                shift = column_sum(block_sum(jnp.where(m, f, 0.0))) / jnp.maximum(held, 1.0)
            apart = jnp.where(m, f - shift, 0.0)
            first = first + block_sum(apart)
            second = second + block_sum(apart * apart)
    first = column_sum(first)
    second = column_sum(second) - first * first / jnp.maximum(count, 1.0)
    first = first + count * shift
    own[0] = packet(first, second, jnp.broadcast_to(count, (1, 256)))
    pl.semaphore_wait(barrier, len(partners))

    def spread_start(stage, devices, boxes, base):
        sent = []
        for j, dev in enumerate(devices):
            cp = copy(own.at[stage], boxes.at[j], st_s.at[base + j], st_r.at[base + j], {"bricks": dev})
            cp.start()
            sent.append(cp)
        return sent

    def spread_end(sent, stage, boxes):
        for cp in sent:
            cp.wait()
        return [own[stage]] + [boxes[j] for j in range(len(sent))]

    sent = spread_start(0, near[1:], got1, 0)

    in_copies[2].wait()
    in_copies[3].wait()
    w_copy.start()
    for s in range(2):
        for j in range(4):
            at = pl.ds(128 * j, 128)
            m = active_rows(s, j)
            fs[2 * c + s, at, :] = jnp.where(m, feat[s, at, :].astype(F32), BIG).astype(BF16)
            zs[2 * c + s, at, :] = jnp.where(m, cot[s, at, :].astype(F32), 0.0).astype(BF16)
    nbv[c] = jnp.zeros((8, 128), jnp.int32)
    nbv[c, 0:2, 0:27] = nbr[...]
    for s in range(2):
        conds[2 * c + s] = jnp.broadcast_to(cond[s : s + 1, :].astype(F32), (8, 256))
    mine = pl.ds(2 * c, 2)
    core_copies = [
        copy(r.at[i], r.at[i], core_s.at[k], core_r.at[k], {"bricks": other})
        for k, (r, i) in enumerate(((nbv, c), (zs, mine), (fs, mine), (conds, mine)))
    ]
    for cp in core_copies:
        cp.start()
    edge_copies = []
    for k, (src, dst, up, down) in enumerate((
        (zs, face_z, pl.ds(448, 64), pl.ds(0, 64)),
        (fs, face_f, pl.ds(448, 64), pl.ds(0, 64)),
        (conds, conds_e, pl.ds(0, 8), pl.ds(0, 8)),
    )):
        for way, (at, dev) in enumerate(((up, after0), (down, before1))):
            cp = copy(
                src.at[mine, at], dst.at[mine], edge_s.at[2 * k + way], edge_r.at[k, c], {"bricks": dev}
            )
            cp.start()
            edge_copies.append(cp)

    def edge_wait(k, dst):
        for core in range(2):
            got = dst.at[pl.ds(2 * core, 2)]
            copy(got, got, edge_s.at[2 * k], edge_r.at[k, core], {"bricks": other}).wait_recv()

    for grid in (hz, zz):
        grid[:, 0:16, :] = jnp.zeros((10, 16, 768), BF16)
        grid[:, 272:288, :] = jnp.zeros((10, 16, 768), BF16)
    fs[4] = jnp.full((512, 256), BIG, BF16)
    zs[4] = jnp.zeros((512, 256), BF16)
    face_f[4] = jnp.full((64, 256), BIG, BF16)
    face_z[4] = jnp.zeros((64, 256), BF16)
    conds[4] = jnp.zeros((8, 256), F32)
    conds_e[4] = jnp.zeros((8, 256), F32)
    wg[pl.ds(LEAD + ROWS, 8), :] = jnp.zeros((8, 256), F32)

    w_copy.wait()

    def turn(g, carry):
        for e in range(3):
            w_back[g, pl.ds(256 * e, 256), :] = w_fwd[8 - g, pl.ds(256 * (2 - e), 256), :].T
        return carry

    lax.fori_loop(0, 9, turn, 0)

    core_copies[0].wait()
    nb_copy = pltpu.make_async_copy(nbv, nbs, nb_sem)
    nb_copy.start()
    nb_copy.wait()
    cy, cz, src, src_e = [], [], [], []
    here = []
    for j in range(4):
        def entry(k):
            return nbs[j // 2, j % 2, k]

        low_y = functools.reduce(jnp.maximum, [entry(9 * a + e) for a in range(3) for e in range(3)])
        low_z = functools.reduce(jnp.maximum, [entry(9 * a + 3 * e) for a in range(3) for e in range(3)])
        cy.append(jnp.where(low_y >= 0, 1, 0))
        cz.append(jnp.where(low_z >= 0, 1, 0))
        here.append(entry(13) >= 0)
    for q in range(4):
        qy, qz = q // 2, q % 2
        at, at_e = jnp.int32(4), jnp.int32(4)
        for j in range(4):
            at = jnp.where(here[j] & (cy[j] == qy) & (cz[j] == qz), j, at)
            t = nbs[j // 2, j % 2, 18 * c + 3 * (qy + 1 - cy[j]) + (qz + 1 - cz[j])]
            at_e = jnp.where(t >= 0, t & 3, at_e)
        src.append(at)
        src_e.append(at_e)

    zi = lax.broadcasted_iota(jnp.int32, (128, 256), 0) & 15

    def joined(left, right):
        pair = [v.reshape(8, 8, 256) for v in (left, right)]
        return jnp.concatenate(pair, axis=1).reshape(128, 256)

    def lay(grid, plane, half, v):
        at = pl.ds(16 + 128 * half, 128)
        grid[plane, at, 0:256] = jnp.where(zi == 0, 0.0, pltpu.roll(v, 1, 0)).astype(BF16)
        grid[plane, at, 256:512] = v.astype(BF16)
        grid[plane, at, 512:768] = jnp.where(zi == 15, 0.0, pltpu.roll(v, 127, 0)).astype(BF16)

    edge_plane = 9 * c

    core_copies[1].wait()

    def lay_z(x, carry):
        for half in range(2):
            at = pl.ds(pl.multiple_of(64 * x, 64), 64)
            v = joined(*[zs[src[2 * half + e], at, :].astype(F32) for e in range(2)])
            lay(zz, x + 1, half, v)
        return carry

    lax.fori_loop(0, 8, lay_z, 0)

    merged = pooled(spread_end(sent, 0, got1))
    own[1] = merged
    sent = spread_start(1, across[1:], got2, 7)

    def conv(grid, taps, acc, kx):
        planes = pl.ds(4 * c + kx, 4)
        lhs = jnp.concatenate([grid[planes, 16 * e : 16 * e + 256, :].reshape(1024, 768) for e in range(3)], axis=1)
        rhs = taps[3 * kx : 3 * kx + 3].reshape(2304, 256)
        made = jnp.dot(lhs, rhs, preferred_element_type=F32).reshape(4, 2, 8, 2, 8, 256)
        acc[...] = made if kx == 1 else acc[...] + made

    conv(zz, w_back, acc_b, 1)
    edge_wait(0, face_z)
    for half in range(2):
        lay(zz, edge_plane, half, joined(*[face_z[src_e[2 * half + e]].astype(F32) for e in range(2)]))
    conv(zz, w_back, acc_b, 0)
    conv(zz, w_back, acc_b, 2)

    merged = pooled(spread_end(sent, 1, got2))
    total = merged[2:3]
    first, second = merged[0:1], merged[1:2]
    total_g = 8.0 * total
    mean = group_sum(first) / total_g
    apart = first / total - mean
    var = group_sum(second + total * apart * apart) / total_g
    inv_std = lax.rsqrt(var + EPSILON)
    gamma = gamma_in[...]
    beta = beta_in[...]
    slope = inv_std * gamma

    for cp in core_copies[2:]:
        cp.wait()
    edge_wait(1, face_f)
    edge_wait(2, conds_e)

    def activation(raw, shift):
        f = raw.astype(F32)
        m = f < LIMIT
        f = jnp.where(m, f, 0.0)
        apart = f - mean
        pre = apart * slope + (beta + shift[0:1])
        sigma = 1.0 / (1.0 + jnp.exp(-pre))
        return m, f, apart, pre, sigma

    def hidden(raw, shift):
        m, _, _, pre, sigma = activation(raw, shift)
        return jnp.where(m, pre * sigma, 0.0)

    def lay_h(x, carry):
        for half in range(2):
            at = pl.ds(pl.multiple_of(64 * x, 64), 64)
            slots = [src[2 * half + e] for e in range(2)]
            lay(hz, x + 1, half, joined(*[hidden(fs[j, at, :], conds[j]) for j in slots]))
        return carry

    lax.fori_loop(0, 8, lay_h, 0)
    for half in range(2):
        slots = [src_e[2 * half + e] for e in range(2)]
        lay(hz, edge_plane, half, joined(*[hidden(face_f[j], conds_e[j]) for j in slots]))

    def taps(low, high):
        def step(i, carry):
            g = 4 * c + i
            at = pl.ds(pl.multiple_of(g % 3 * 16, 16), 256)
            lhs = hz[pl.ds(g // 3, 8), at, :].reshape(2048, 768)
            center = zz[1:9, 16:272, 256:512].reshape(2048, 256)
            wg[pl.ds(pl.multiple_of(LEAD * (1 - c) + 768 * i, 128), 768), :] = lax.dot_general(
                lhs, center, (((0,), (0,)), ((), ())), preferred_element_type=F32
            )
            return carry

        lax.fori_loop(low, high, step, 0)

    way = ((8, 2), (2, 8))
    place = ((xm, ym), (ym, xm))

    def deal(h):
        def step(x, carry):
            base = pl.multiple_of(LEAD + 864 * h + 216 * x, 8)
            for y in range(4):
                low = 54 * y // 8 * 8
                v = wg[pl.ds(base + low, 64), :][54 * y - low : 54 * y - low + 54]
                part[0, x, h, y] = v[:, 0:128]
                part[1, y, h, x] = v[:, 128:256]
            return carry

        lax.fori_loop(0, 4, step, 0)

    live = {}

    def first_start(h):
        for k in range(2):
            a = place[k][0]
            for e, step in ((0, 1), (1, 3)):
                cp = copy(
                    part.at[k, (a + 2) % 4, h, pl.ds(2 * e, 2)], r1.at[k, h, e],
                    rs1_s.at[k, h, e], rs1_r.at[k, h, e], {"bricks": moved(b, way[k][0], 4, step)},
                )
                cp.start()
                live[1, k, h, e] = cp

    def second_start(h):
        for k in range(2):
            a = place[k][0]
            for e, step in ((0, 1), (1, 3)):
                live[1, k, h, e].wait()
                to = (a + step) % 4
                part[k, to, h, pl.ds(2 * e, 2)] += r1[k, h, e]
                cp = copy(
                    part.at[k, to, h], r2.at[k, h, e], rs2_s.at[k, h, e], rs2_r.at[k, h, e],
                    {"bricks": moved(b, way[k][0], 4, step)},
                )
                cp.start()
                live[2, k, h, e] = cp

    def third_start(h):
        for k in range(2):
            a, at = place[k]
            for e in range(2):
                live[2, k, h, e].wait()
            part[k, a, h] += r2[k, h, 0] + r2[k, h, 1]
            for j in range(1, 4):
                cp = copy(
                    part.at[k, a, h, (at + j) % 4], r3.at[k, h, j - 1], rs3_s.at[k, h, j - 1], rs3_r.at[k, h, j - 1],
                    {"bricks": moved(b, way[k][1], 4, j)},
                )
                cp.start()
                live[3, k, h, j] = cp

    side = jnp.where(c == d, 0, 1)

    def window(core):
        return pl.ds(pl.multiple_of(24 * core, 8), 30)

    def to_self(h):
        return (c == d) & (hm == h)

    def z_copies(h):
        one, two = [], []
        for k in range(2):
            a, at = place[k]
            base = b % 32 + 32 * h
            for group, core, dev in ((one, 1 - c, base + 1 - 2 * c), (two, c, base)):
                group.append(copy(
                    part.at[k, a, h, at, window(core)], zr.at[side, hm, k],
                    z_s.at[h, len(group), k], z_r.at[side, hm, k], {"dp": c, "bricks": dev},
                ))
        return one, two

    def z_start(h):
        for k in range(2):
            a, at = place[k]
            for j in range(1, 4):
                live[3, k, h, j].wait()
            part[k, a, h, at] += r3[k, h, 0] + r3[k, h, 1] + r3[k, h, 2]
        one, two = z_copies(h)
        for cp in one:
            cp.start()

        @pl.when(jnp.logical_not(to_self(h)))
        def _():
            for cp in two:
                cp.start()

        @pl.when(to_self(h))
        def _():
            for k in range(2):
                a, at = place[k]
                zr[0, h, k] = part[k, a, h, at, window(c), :]

    def z_end():
        for h in range(4):
            one, two = z_copies(h)
            for cp in one:
                cp.wait_send()

            @pl.when(jnp.logical_not(to_self(h)))
            def _():
                for cp in two:
                    cp.wait_send()
                for k in range(2):
                    copy(zr.at[0, h, k], zr.at[0, h, k], z_s.at[h, 0, k], z_r.at[0, h, k], {"bricks": other}).wait_recv()

            for k in range(2):
                copy(zr.at[1, h, k], zr.at[1, h, k], z_s.at[h, 0, k], z_r.at[1, h, k], {"bricks": other}).wait_recv()
        for k in range(2):
            v = sum(zr[e, h, k] for e in range(2) for h in range(4))
            wgrad[pl.ds(k, 27, stride=2), :] = jnp.where(c == 0, v[0:27], v[3:30])

    def slot_block(j, plane):
        at = pl.ds(pl.multiple_of(256 * c + 64 * plane, 64), 64)
        return at, activation(fs[j, at, :], conds[j])

    def back_pass(plane, carry):
        one, two = carry
        for j in range(4):
            at, (m, f, apart, pre, sigma) = slot_block(j, plane)
            back = acc_b[plane, cy[j], :, cz[j]].reshape(64, 256)
            sg = jnp.where(m, gamma * back * sigma * (1.0 + pre * (1.0 - sigma)), 0.0)
            sg_s[j, plane] = sg
            one = one + block_sum(sg)
            two = two + block_sum(sg * (apart * inv_std))
        return one, two

    def back_start():
        zero = jnp.zeros((8, 256), F32)
        one, two = lax.fori_loop(0, 4, back_pass, (zero, zero))
        own[2] = packet(column_sum(one), column_sum(two))
        return spread_start(2, across[1:], back1, 22)

    def out_pass(plane, carry):
        for j in range(4):
            at = pl.ds(pl.multiple_of(256 * c + 64 * plane, 64), 64)
            f = fs[j, at, :].astype(F32)
            made = acc_f[plane, cy[j], :, cz[j]].reshape(64, 256)
            outs[j, at, :] = jnp.where(f < LIMIT, f + made, 0.0).astype(BF16)
        return carry

    theirs = pl.ds(2 - 2 * c, 2)
    half_rows = pl.ds(pl.multiple_of(256 * c, 256), 256)

    def hand_over(ref, k):
        piece = ref.at[theirs, half_rows]
        cp = copy(piece, piece, res_s.at[k], res_r.at[k], {"bricks": other})
        cp.start()
        return cp

    def grad_pass(grad_mean, cross_mean, plane, carry):
        for j in range(4):
            at = pl.ds(pl.multiple_of(256 * c + 64 * plane, 64), 64)
            f = fs[j, at, :].astype(F32)
            x_hat = (f - mean) * inv_std
            v = inv_std * (sg_s[j, plane] - grad_mean - x_hat * cross_mean) + zs[j, at, :].astype(F32)
            grads[j, at, :] = jnp.where(f < LIMIT, v, 0.0).astype(BF16)
        return carry

    for h in range(4):
        taps(CUTS[h], CUTS[h + 1])
        deal(h)
        first_start(h)
        if h == 0:
            sent = back_start()
        if h >= 1:
            second_start(h - 1)
    own[3] = sum(spread_end(sent, 2, back1))
    sent = spread_start(3, near[1:], back2, 37)
    conv(hz, w_fwd, acc_f, 1)
    second_start(3)
    third_start(0)
    conv(hz, w_fwd, acc_f, 0)
    third_start(1)
    sums = sum(spread_end(sent, 3, back2))
    grad_mean = group_sum(sums[0:1]) / total_g
    cross_mean = group_sum(sums[1:2]) / total_g
    lax.fori_loop(0, 4, functools.partial(grad_pass, grad_mean, cross_mean), 0)
    grad_copy = hand_over(grads, 1)
    third_start(2)
    conv(hz, w_fwd, acc_f, 2)
    lax.fori_loop(0, 4, out_pass, 0)
    out_copy = hand_over(outs, 0)
    z_start(0)
    third_start(3)
    z_start(1)
    z_start(2)
    stores = []
    for k, (cp, ref, to) in enumerate(((out_copy, outs, out), (grad_copy, grads, fgrad))):
        cp.wait()
        stores.append(pltpu.make_async_copy(ref.at[mine], to, out_sem.at[k]))
        stores[k].start()
    z_start(3)
    for cp in edge_copies:
        cp.wait_send()
    for cp in stores:
        cp.wait()
    z_end()


def hand_out(*refs):
    sources, targets, held, sem_in, sem_out = refs[:3], refs[3:6], refs[6:9], refs[9], refs[10]
    steps = []
    for i in range(3):
        rows = sources[i].shape[0]
        for k in range(1 if i == 2 else rows):
            at = pl.ds(0, rows) if i == 2 else pl.ds(k, 1)
            steps.append((
                pltpu.make_async_copy(sources[i].at[at], held[i].at[at], sem_in.at[i, k]),
                pltpu.make_async_copy(held[i].at[at], targets[i].at[at], sem_out.at[i, k]),
            ))
    for load, _ in steps:
        load.start()
    for load, store in steps:
        load.wait()
        store.start()
    for _, store in steps:
        store.wait()


def on_device(features, active, neighbours, cond, gamma, beta, weight, cotangent):
    vmem = pl.BlockSpec(memory_space=pltpu.VMEM)
    dma = pltpu.SemaphoreType.DMA
    scratch = [
        pltpu.VMEM((2, 512, 256), BF16),
        pltpu.VMEM((2, 512, 256), BF16),
        pltpu.VMEM((5, 512, 256), BF16),
        pltpu.VMEM((5, 512, 256), BF16),
        pltpu.VMEM((5, 64, 256), BF16),
        pltpu.VMEM((5, 64, 256), BF16),
        pltpu.VMEM((5, 8, 256), F32),
        pltpu.VMEM((5, 8, 256), F32),
        pltpu.VMEM((2, 8, 128), jnp.int32),
        pltpu.SMEM((2, 8, 128), jnp.int32),
        pltpu.VMEM((9, 768, 256), BF16),
        pltpu.VMEM((9, 768, 256), BF16),
        pltpu.VMEM((10, 288, 768), BF16),
        pltpu.VMEM((10, 288, 768), BF16),
        pltpu.VMEM((LEAD + 3840, 256), F32),
        pltpu.VMEM((2, 4, 4, 4, 54, 128), F32),
        pltpu.VMEM((2, 4, 2, 2, 54, 128), F32),
        pltpu.VMEM((2, 4, 2, 4, 54, 128), F32),
        pltpu.VMEM((2, 4, 3, 54, 128), F32),
        pltpu.VMEM((2, 4, 2, 30, 128), F32),
        pltpu.VMEM((4, 2, 8, 2, 8, 256), F32),
        pltpu.VMEM((4, 2, 8, 2, 8, 256), F32),
        pltpu.VMEM((4, 4, 64, 256), F32),
        pltpu.VMEM((4, 512, 256), BF16),
        pltpu.VMEM((4, 512, 256), BF16),
        pltpu.VMEM((4, 8, 256), F32),
        pltpu.VMEM((7, 8, 256), F32),
        pltpu.VMEM((15, 8, 256), F32),
        pltpu.VMEM((15, 8, 256), F32),
        pltpu.VMEM((7, 8, 256), F32),
        dma, dma, dma((4,)), dma((4,)), dma((6,)), dma((3, 2)), dma((44,)), dma((44,)),
        dma((2, 4, 2)), dma((2, 4, 2)), dma((2, 4, 2)), dma((2, 4, 2)),
        dma((2, 4, 3)), dma((2, 4, 3)), dma((4, 2, 2)), dma((2, 4, 2)),
        dma((2,)), dma((2,)), dma((2, 2)), dma((2,)),
    ]
    shapes = (
        jax.ShapeDtypeStruct((2, 512, 256), BF16),
        jax.ShapeDtypeStruct((2, 512, 256), BF16),
        jax.ShapeDtypeStruct((54, 128), F32),
    )
    anywhere = pl.BlockSpec(memory_space=pl.ANY)
    made = pl.pallas_call(
        kernel,
        out_shape=shapes,
        in_specs=[anywhere] * 2 + [vmem] * 5 + [anywhere],
        out_specs=(anywhere, anywhere, vmem),
        scratch_shapes=scratch,
        compiler_params=pltpu.CompilerParams(
            collective_id=0, has_side_effects=True, vmem_limit_bytes=60 * 2**20
        ),
        name="layer",
    )(
        features[0], cotangent[0], active[0], neighbours[0], cond[0],
        gamma.reshape(1, 256), beta.reshape(1, 256), weight.reshape(9, 768, 256),
    )
    output, feature_grad, weight_grad = pl.pallas_call(
        hand_out, out_shape=shapes, in_specs=[anywhere] * 3, out_specs=(anywhere,) * 3,
        scratch_shapes=[pltpu.VMEM(v.shape, v.dtype) for v in shapes] + [dma((3, 2)), dma((3, 2))],
        compiler_params=pltpu.CompilerParams(vmem_limit_bytes=60 * 2**20), name="hand_out",
    )(*made)
    return output[None], feature_grad[None], weight_grad.reshape(-1)


def solution(mesh):
    whole = P("dp", "bricks", None, None)
    rows = P("dp", "bricks", None)
    return jax.shard_map(
        on_device, mesh=mesh, in_specs=(whole, rows, rows, rows, P(), P(), P(), whole),
        out_specs=(whole, whole, P(("dp", "bricks"))), check_vma=False,
    )
```

```python
import functools

import jax
import jax.numpy as jnp
from jax import lax
from jax.experimental import pallas as pl
from jax.experimental.pallas import tpu as pltpu
from jax.sharding import PartitionSpec as P

MESH = pl.DeviceIdType.MESH
F32 = jnp.float32
BF16 = jnp.bfloat16
EPSILON = 1e-05
BIG = 1e30
LIMIT = 1e29
LAYERS = 64
ROWS = 3456
CUTS = (0, 2, 3, 4, 5)
LEAD = 384


def moved(index, stride, size, step):
    digit = (index // stride) % size
    return index + ((digit + step) % size - digit) * stride


def block_sum(v):
    return jnp.sum(v.reshape(v.shape[0] // 8, 8, v.shape[1]), axis=0)


def column_sum(v):
    return jnp.sum(v, axis=0, keepdims=True)


def packet(*rows):
    place = lax.broadcasted_iota(jnp.int32, (8, 256), 0)
    out = jnp.zeros((8, 256), F32)
    for i, row in enumerate(rows):
        out = jnp.where(place == i, row, out)
    return out


def pooled(parts):
    count = sum(p[2:3] for p in parts)
    first = sum(p[0:1] for p in parts)
    mean = first / jnp.maximum(count, 1.0)
    second = sum(p[1:2] for p in parts)
    for p in parts:
        apart = p[0:1] / jnp.maximum(p[2:3], 1.0) - mean
        second = second + p[2:3] * apart * apart
    return packet(first, second, count)


def group_sum(row):
    v = jnp.broadcast_to(row, (8, 256))
    lane = lax.broadcasted_iota(jnp.int32, (8, 256), 1)
    for step in (1, 2, 4):
        up = pltpu.roll(v, 256 - step, 1)
        down = pltpu.roll(v, step, 1)
        v = v + jnp.where((lane & step) == 0, up, down)
    return v[0:1]


def kernel(
    feat_hbm, cot_hbm, act, nbr, cond, gamma_in, beta_in, w_hbm,
    out, fgrad, wgrad,
    feat, cot, fs, zs, face_f, face_z, conds, conds_e, nbv, nbs,
    w_fwd, w_back, hz, zz, wg, part, r1, r2, r3, zr,
    acc_f, acc_b, sg_s, outs, grads,
    own, got1, got2, back1, back2,
    w_sem, nb_sem, core_s, core_r, edge_s, edge_r, st_s, st_r, rs1_s, rs1_r, rs2_s, rs2_r, rs3_s, rs3_r, z_s, z_r,
    res_s, res_r, in_sem, out_sem,
):
    d = lax.axis_index("dp")
    b = lax.axis_index("bricks")
    c = b % 2
    layer = b // 2
    xm = (b // 8) % 4
    ym = (b // 2) % 4
    hm = b // 32
    after0 = ((layer + 1) % LAYERS) * 2
    before1 = ((layer + LAYERS - 1) % LAYERS) * 2 + 1
    beside = jnp.where(c == 0, (layer + LAYERS - 1) % LAYERS, (layer + 1) % LAYERS) * 2

    def copy(src, dst, ssem, rsem, dev):
        return pltpu.make_async_remote_copy(
            src_ref=src, dst_ref=dst, send_sem=ssem, recv_sem=rsem, device_id=dev, device_id_type=MESH
        )

    w_copy = pltpu.make_async_copy(w_hbm, w_fwd, w_sem)

    barrier = pltpu.get_barrier_semaphore()
    other = b + 1 - 2 * c
    near = []
    for j in range(4):
        up = moved(b, 32, 4, j)
        near += [up, up + 1 - 2 * c]
    across = [moved(moved(b, 8, 4, j), 2, 4, i) for j in range(4) for i in range(4)]
    partners = [{"dp": 1 - d, "bricks": dev} for dev in near]
    partners += [{"bricks": dev} for dev in near[1:] + across[1:]]
    partners += [{"bricks": after0}, {"bricks": before1}, {"bricks": beside}, {"bricks": beside + 1}]
    for dev in partners:
        pl.semaphore_signal(barrier, inc=1, device_id=dev, device_id_type=MESH)
    in_copies = []
    for k, (src, dst) in enumerate(((feat_hbm, feat), (cot_hbm, cot))):
        for s in range(2):
            cp = pltpu.make_async_copy(src.at[s], dst.at[s], in_sem.at[s, k])
            cp.start()
            in_copies.append(cp)

    rows = [act[s : s + 1, 128 * j : 128 * j + 128] for s in range(2) for j in range(4)]
    flags = jnp.concatenate(rows, axis=0).astype(F32)
    count = jnp.sum(jnp.sum(flags, axis=1, keepdims=True), axis=0, keepdims=True)
    flags_t = flags.T
    def active_rows(s, j):
        return jnp.broadcast_to(flags_t[:, 4 * s + j : 4 * s + j + 1], (128, 256)) > 0.5

    shift = None
    first = jnp.zeros((8, 256), F32)
    second = jnp.zeros((8, 256), F32)
    for s in range(2):
        in_copies[s].wait()
        for j in range(4):
            m = active_rows(s, j)
            f = feat[s, pl.ds(128 * j, 128), :].astype(F32)
            if shift is None:
                held = column_sum(block_sum(jnp.where(m, 1.0, 0.0)))
                shift = column_sum(block_sum(jnp.where(m, f, 0.0))) / jnp.maximum(held, 1.0)
            apart = jnp.where(m, f - shift, 0.0)
            first = first + block_sum(apart)
            second = second + block_sum(apart * apart)
    first = column_sum(first)
    second = column_sum(second) - first * first / jnp.maximum(count, 1.0)
    first = first + count * shift
    own[0] = packet(first, second, jnp.broadcast_to(count, (1, 256)))
    pl.semaphore_wait(barrier, len(partners))

    def spread_start(stage, devices, boxes, base):
        sent = []
        for j, dev in enumerate(devices):
            cp = copy(own.at[stage], boxes.at[j], st_s.at[base + j], st_r.at[base + j], {"bricks": dev})
            cp.start()
            sent.append(cp)
        return sent

    def spread_end(sent, stage, boxes):
        for cp in sent:
            cp.wait()
        return [own[stage]] + [boxes[j] for j in range(len(sent))]

    sent = spread_start(0, near[1:], got1, 0)

    in_copies[2].wait()
    in_copies[3].wait()
    w_copy.start()
    for s in range(2):
        for j in range(4):
            at = pl.ds(128 * j, 128)
            m = active_rows(s, j)
            fs[2 * c + s, at, :] = jnp.where(m, feat[s, at, :].astype(F32), BIG).astype(BF16)
            zs[2 * c + s, at, :] = jnp.where(m, cot[s, at, :].astype(F32), 0.0).astype(BF16)
    nbv[c] = jnp.zeros((8, 128), jnp.int32)
    nbv[c, 0:2, 0:27] = nbr[...]
    for s in range(2):
        conds[2 * c + s] = jnp.broadcast_to(cond[s : s + 1, :].astype(F32), (8, 256))
    mine = pl.ds(2 * c, 2)
    core_copies = [
        copy(r.at[i], r.at[i], core_s.at[k], core_r.at[k], {"bricks": other})
        for k, (r, i) in enumerate(((nbv, c), (zs, mine), (fs, mine), (conds, mine)))
    ]
    for cp in core_copies:
        cp.start()
    edge_copies = []
    for k, (src, dst, up, down) in enumerate((
        (zs, face_z, pl.ds(448, 64), pl.ds(0, 64)),
        (fs, face_f, pl.ds(448, 64), pl.ds(0, 64)),
        (conds, conds_e, pl.ds(0, 8), pl.ds(0, 8)),
    )):
        for way, (at, dev) in enumerate(((up, after0), (down, before1))):
            cp = copy(
                src.at[mine, at], dst.at[mine], edge_s.at[2 * k + way], edge_r.at[k, c], {"bricks": dev}
            )
            cp.start()
            edge_copies.append(cp)

    def edge_wait(k, dst):
        for core in range(2):
            got = dst.at[pl.ds(2 * core, 2)]
            copy(got, got, edge_s.at[2 * k], edge_r.at[k, core], {"bricks": other}).wait_recv()

    for grid in (hz, zz):
        grid[:, 0:16, :] = jnp.zeros((10, 16, 768), BF16)
        grid[:, 272:288, :] = jnp.zeros((10, 16, 768), BF16)
    fs[4] = jnp.full((512, 256), BIG, BF16)
    zs[4] = jnp.zeros((512, 256), BF16)
    face_f[4] = jnp.full((64, 256), BIG, BF16)
    face_z[4] = jnp.zeros((64, 256), BF16)
    conds[4] = jnp.zeros((8, 256), F32)
    conds_e[4] = jnp.zeros((8, 256), F32)
    wg[pl.ds(LEAD + ROWS, 8), :] = jnp.zeros((8, 256), F32)

    w_copy.wait()

    def turn(g, carry):
        for e in range(3):
            w_back[g, pl.ds(256 * e, 256), :] = w_fwd[8 - g, pl.ds(256 * (2 - e), 256), :].T
        return carry

    lax.fori_loop(0, 9, turn, 0)

    core_copies[0].wait()
    nb_copy = pltpu.make_async_copy(nbv, nbs, nb_sem)
    nb_copy.start()
    nb_copy.wait()
    cy, cz, src, src_e = [], [], [], []
    here = []
    for j in range(4):
        def entry(k):
            return nbs[j // 2, j % 2, k]

        low_y = functools.reduce(jnp.maximum, [entry(9 * a + e) for a in range(3) for e in range(3)])
        low_z = functools.reduce(jnp.maximum, [entry(9 * a + 3 * e) for a in range(3) for e in range(3)])
        cy.append(jnp.where(low_y >= 0, 1, 0))
        cz.append(jnp.where(low_z >= 0, 1, 0))
        here.append(entry(13) >= 0)
    for q in range(4):
        qy, qz = q // 2, q % 2
        at, at_e = jnp.int32(4), jnp.int32(4)
        for j in range(4):
            at = jnp.where(here[j] & (cy[j] == qy) & (cz[j] == qz), j, at)
            t = nbs[j // 2, j % 2, 18 * c + 3 * (qy + 1 - cy[j]) + (qz + 1 - cz[j])]
            at_e = jnp.where(t >= 0, t & 3, at_e)
        src.append(at)
        src_e.append(at_e)

    zi = lax.broadcasted_iota(jnp.int32, (128, 256), 0) & 15

    def joined(left, right):
        pair = [v.reshape(8, 8, 256) for v in (left, right)]
        return jnp.concatenate(pair, axis=1).reshape(128, 256)

    def lay(grid, plane, half, v):
        at = pl.ds(16 + 128 * half, 128)
        grid[plane, at, 0:256] = jnp.where(zi == 0, 0.0, pltpu.roll(v, 1, 0)).astype(BF16)
        grid[plane, at, 256:512] = v.astype(BF16)
        grid[plane, at, 512:768] = jnp.where(zi == 15, 0.0, pltpu.roll(v, 127, 0)).astype(BF16)

    edge_plane = 9 * c

    core_copies[1].wait()

    def lay_z(x, carry):
        for half in range(2):
            at = pl.ds(pl.multiple_of(64 * x, 64), 64)
            v = joined(*[zs[src[2 * half + e], at, :].astype(F32) for e in range(2)])
            lay(zz, x + 1, half, v)
        return carry

    lax.fori_loop(0, 8, lay_z, 0)

    merged = pooled(spread_end(sent, 0, got1))
    own[1] = merged
    sent = spread_start(1, across[1:], got2, 7)

    def conv(grid, taps, acc, kx):
        planes = pl.ds(4 * c + kx, 4)
        lhs = jnp.concatenate([grid[planes, 16 * e : 16 * e + 256, :].reshape(1024, 768) for e in range(3)], axis=1)
        rhs = taps[3 * kx : 3 * kx + 3].reshape(2304, 256)
        made = jnp.dot(lhs, rhs, preferred_element_type=F32).reshape(4, 2, 8, 2, 8, 256)
        acc[...] = made if kx == 1 else acc[...] + made

    conv(zz, w_back, acc_b, 1)
    edge_wait(0, face_z)
    for half in range(2):
        lay(zz, edge_plane, half, joined(*[face_z[src_e[2 * half + e]].astype(F32) for e in range(2)]))
    conv(zz, w_back, acc_b, 0)
    conv(zz, w_back, acc_b, 2)

    merged = pooled(spread_end(sent, 1, got2))
    total = merged[2:3]
    first, second = merged[0:1], merged[1:2]
    total_g = 8.0 * total
    mean = group_sum(first) / total_g
    apart = first / total - mean
    var = group_sum(second + total * apart * apart) / total_g
    inv_std = lax.rsqrt(var + EPSILON)
    gamma = gamma_in[...]
    beta = beta_in[...]
    slope = inv_std * gamma

    for cp in core_copies[2:]:
        cp.wait()
    edge_wait(1, face_f)
    edge_wait(2, conds_e)

    def activation(raw, shift):
        f = raw.astype(F32)
        m = f < LIMIT
        f = jnp.where(m, f, 0.0)
        apart = f - mean
        pre = apart * slope + (beta + shift[0:1])
        sigma = 1.0 / (1.0 + jnp.exp(-pre))
        return m, f, apart, pre, sigma

    def hidden(raw, shift):
        m, _, _, pre, sigma = activation(raw, shift)
        return jnp.where(m, pre * sigma, 0.0)

    def lay_h(x, carry):
        for half in range(2):
            at = pl.ds(pl.multiple_of(64 * x, 64), 64)
            slots = [src[2 * half + e] for e in range(2)]
            lay(hz, x + 1, half, joined(*[hidden(fs[j, at, :], conds[j]) for j in slots]))
        return carry

    lax.fori_loop(0, 8, lay_h, 0)
    for half in range(2):
        slots = [src_e[2 * half + e] for e in range(2)]
        lay(hz, edge_plane, half, joined(*[hidden(face_f[j], conds_e[j]) for j in slots]))

    def taps(low, high):
        def step(i, carry):
            g = 4 * c + i
            at = pl.ds(pl.multiple_of(g % 3 * 16, 16), 256)
            lhs = hz[pl.ds(g // 3, 8), at, :].reshape(2048, 768)
            center = zz[1:9, 16:272, 256:512].reshape(2048, 256)
            wg[pl.ds(pl.multiple_of(LEAD * (1 - c) + 768 * i, 128), 768), :] = lax.dot_general(
                lhs, center, (((0,), (0,)), ((), ())), preferred_element_type=F32
            )
            return carry

        lax.fori_loop(low, high, step, 0)

    way = ((8, 2), (2, 8))
    place = ((xm, ym), (ym, xm))

    def deal(h):
        def step(x, carry):
            base = pl.multiple_of(LEAD + 864 * h + 216 * x, 8)
            for y in range(4):
                low = 54 * y // 8 * 8
                v = wg[pl.ds(base + low, 64), :][54 * y - low : 54 * y - low + 54]
                part[0, x, h, y] = v[:, 0:128]
                part[1, y, h, x] = v[:, 128:256]
            return carry

        lax.fori_loop(0, 4, step, 0)

    live = {}

    def first_start(h):
        for k in range(2):
            a = place[k][0]
            for e, step in ((0, 1), (1, 3)):
                cp = copy(
                    part.at[k, (a + 2) % 4, h, pl.ds(2 * e, 2)], r1.at[k, h, e],
                    rs1_s.at[k, h, e], rs1_r.at[k, h, e], {"bricks": moved(b, way[k][0], 4, step)},
                )
                cp.start()
                live[1, k, h, e] = cp

    def second_start(h):
        for k in range(2):
            a = place[k][0]
            for e, step in ((0, 1), (1, 3)):
                live[1, k, h, e].wait()
                to = (a + step) % 4
                part[k, to, h, pl.ds(2 * e, 2)] += r1[k, h, e]
                cp = copy(
                    part.at[k, to, h], r2.at[k, h, e], rs2_s.at[k, h, e], rs2_r.at[k, h, e],
                    {"bricks": moved(b, way[k][0], 4, step)},
                )
                cp.start()
                live[2, k, h, e] = cp

    def third_start(h):
        for k in range(2):
            a, at = place[k]
            for e in range(2):
                live[2, k, h, e].wait()
            part[k, a, h] += r2[k, h, 0] + r2[k, h, 1]
            for j in range(1, 4):
                cp = copy(
                    part.at[k, a, h, (at + j) % 4], r3.at[k, h, j - 1], rs3_s.at[k, h, j - 1], rs3_r.at[k, h, j - 1],
                    {"bricks": moved(b, way[k][1], 4, j)},
                )
                cp.start()
                live[3, k, h, j] = cp

    side = jnp.where(c == d, 0, 1)

    def window(core):
        return pl.ds(pl.multiple_of(24 * core, 8), 30)

    def to_self(h):
        return (c == d) & (hm == h)

    def z_copies(h):
        one, two = [], []
        for k in range(2):
            a, at = place[k]
            base = b % 32 + 32 * h
            for group, core, dev in ((one, 1 - c, base + 1 - 2 * c), (two, c, base)):
                group.append(copy(
                    part.at[k, a, h, at, window(core)], zr.at[side, hm, k],
                    z_s.at[h, len(group), k], z_r.at[side, hm, k], {"dp": c, "bricks": dev},
                ))
        return one, two

    def z_start(h):
        for k in range(2):
            a, at = place[k]
            for j in range(1, 4):
                live[3, k, h, j].wait()
            part[k, a, h, at] += r3[k, h, 0] + r3[k, h, 1] + r3[k, h, 2]
        one, two = z_copies(h)
        for cp in one:
            cp.start()

        @pl.when(jnp.logical_not(to_self(h)))
        def _():
            for cp in two:
                cp.start()

        @pl.when(to_self(h))
        def _():
            for k in range(2):
                a, at = place[k]
                zr[0, h, k] = part[k, a, h, at, window(c), :]

    def z_end():
        for h in range(4):
            one, two = z_copies(h)
            for cp in one:
                cp.wait_send()

            @pl.when(jnp.logical_not(to_self(h)))
            def _():
                for cp in two:
                    cp.wait_send()
                for k in range(2):
                    copy(zr.at[0, h, k], zr.at[0, h, k], z_s.at[h, 0, k], z_r.at[0, h, k], {"bricks": other}).wait_recv()

            for k in range(2):
                copy(zr.at[1, h, k], zr.at[1, h, k], z_s.at[h, 0, k], z_r.at[1, h, k], {"bricks": other}).wait_recv()
        for k in range(2):
            v = sum(zr[e, h, k] for e in range(2) for h in range(4))
            wgrad[pl.ds(k, 27, stride=2), :] = jnp.where(c == 0, v[0:27], v[3:30])

    def slot_block(j, plane):
        at = pl.ds(pl.multiple_of(256 * c + 64 * plane, 64), 64)
        return at, activation(fs[j, at, :], conds[j])

    def back_pass(plane, carry):
        one, two = carry
        for j in range(4):
            at, (m, f, apart, pre, sigma) = slot_block(j, plane)
            back = acc_b[plane, cy[j], :, cz[j]].reshape(64, 256)
            sg = jnp.where(m, gamma * back * sigma * (1.0 + pre * (1.0 - sigma)), 0.0)
            sg_s[j, plane] = sg
            one = one + block_sum(sg)
            two = two + block_sum(sg * (apart * inv_std))
        return one, two

    def back_start():
        zero = jnp.zeros((8, 256), F32)
        one, two = lax.fori_loop(0, 4, back_pass, (zero, zero))
        own[2] = packet(column_sum(one), column_sum(two))
        return spread_start(2, across[1:], back1, 22)

    def out_pass(plane, carry):
        for j in range(4):
            at = pl.ds(pl.multiple_of(256 * c + 64 * plane, 64), 64)
            f = fs[j, at, :].astype(F32)
            made = acc_f[plane, cy[j], :, cz[j]].reshape(64, 256)
            outs[j, at, :] = jnp.where(f < LIMIT, f + made, 0.0).astype(BF16)
        return carry

    theirs = pl.ds(2 - 2 * c, 2)
    half_rows = pl.ds(pl.multiple_of(256 * c, 256), 256)

    def hand_over(ref, k):
        piece = ref.at[theirs, half_rows]
        cp = copy(piece, piece, res_s.at[k], res_r.at[k], {"bricks": other})
        cp.start()
        return cp

    def grad_pass(grad_mean, cross_mean, plane, carry):
        for j in range(4):
            at = pl.ds(pl.multiple_of(256 * c + 64 * plane, 64), 64)
            f = fs[j, at, :].astype(F32)
            x_hat = (f - mean) * inv_std
            v = inv_std * (sg_s[j, plane] - grad_mean - x_hat * cross_mean) + zs[j, at, :].astype(F32)
            grads[j, at, :] = jnp.where(f < LIMIT, v, 0.0).astype(BF16)
        return carry

    for h in range(4):
        taps(CUTS[h], CUTS[h + 1])
        deal(h)
        first_start(h)
        if h == 0:
            sent = back_start()
        if 1 <= h <= 2:
            second_start(h - 1)
    own[3] = sum(spread_end(sent, 2, back1))
    sent = spread_start(3, near[1:], back2, 37)
    conv(hz, w_fwd, acc_f, 1)
    third_start(0)
    second_start(2)
    conv(hz, w_fwd, acc_f, 0)
    third_start(1)
    second_start(3)
    sums = sum(spread_end(sent, 3, back2))
    grad_mean = group_sum(sums[0:1]) / total_g
    cross_mean = group_sum(sums[1:2]) / total_g
    lax.fori_loop(0, 4, functools.partial(grad_pass, grad_mean, cross_mean), 0)
    grad_copy = hand_over(grads, 1)
    third_start(2)
    z_start(0)
    conv(hz, w_fwd, acc_f, 2)
    lax.fori_loop(0, 4, out_pass, 0)
    out_copy = hand_over(outs, 0)
    third_start(3)
    z_start(1)
    z_start(2)
    stores = []
    for k, (cp, ref, to) in enumerate(((out_copy, outs, out), (grad_copy, grads, fgrad))):
        cp.wait()
        stores.append(pltpu.make_async_copy(ref.at[mine], to, out_sem.at[k]))
        stores[k].start()
    z_start(3)
    for cp in edge_copies:
        cp.wait_send()
    for cp in stores:
        cp.wait()
    z_end()


def hand_out(*refs):
    sources, targets, held, sem_in, sem_out = refs[:3], refs[3:6], refs[6:9], refs[9], refs[10]
    steps = []
    for i in range(3):
        rows = sources[i].shape[0]
        for k in range(1 if i == 2 else rows):
            at = pl.ds(0, rows) if i == 2 else pl.ds(k, 1)
            steps.append((
                pltpu.make_async_copy(sources[i].at[at], held[i].at[at], sem_in.at[i, k]),
                pltpu.make_async_copy(held[i].at[at], targets[i].at[at], sem_out.at[i, k]),
            ))
    for load, _ in steps:
        load.start()
    for load, store in steps:
        load.wait()
        store.start()
    for _, store in steps:
        store.wait()


def on_device(features, active, neighbours, cond, gamma, beta, weight, cotangent):
    vmem = pl.BlockSpec(memory_space=pltpu.VMEM)
    dma = pltpu.SemaphoreType.DMA
    scratch = [
        pltpu.VMEM((2, 512, 256), BF16),
        pltpu.VMEM((2, 512, 256), BF16),
        pltpu.VMEM((5, 512, 256), BF16),
        pltpu.VMEM((5, 512, 256), BF16),
        pltpu.VMEM((5, 64, 256), BF16),
        pltpu.VMEM((5, 64, 256), BF16),
        pltpu.VMEM((5, 8, 256), F32),
        pltpu.VMEM((5, 8, 256), F32),
        pltpu.VMEM((2, 8, 128), jnp.int32),
        pltpu.SMEM((2, 8, 128), jnp.int32),
        pltpu.VMEM((9, 768, 256), BF16),
        pltpu.VMEM((9, 768, 256), BF16),
        pltpu.VMEM((10, 288, 768), BF16),
        pltpu.VMEM((10, 288, 768), BF16),
        pltpu.VMEM((LEAD + 3840, 256), F32),
        pltpu.VMEM((2, 4, 4, 4, 54, 128), F32),
        pltpu.VMEM((2, 4, 2, 2, 54, 128), F32),
        pltpu.VMEM((2, 4, 2, 4, 54, 128), F32),
        pltpu.VMEM((2, 4, 3, 54, 128), F32),
        pltpu.VMEM((2, 4, 2, 30, 128), F32),
        pltpu.VMEM((4, 2, 8, 2, 8, 256), F32),
        pltpu.VMEM((4, 2, 8, 2, 8, 256), F32),
        pltpu.VMEM((4, 4, 64, 256), F32),
        pltpu.VMEM((4, 512, 256), BF16),
        pltpu.VMEM((4, 512, 256), BF16),
        pltpu.VMEM((4, 8, 256), F32),
        pltpu.VMEM((7, 8, 256), F32),
        pltpu.VMEM((15, 8, 256), F32),
        pltpu.VMEM((15, 8, 256), F32),
        pltpu.VMEM((7, 8, 256), F32),
        dma, dma, dma((4,)), dma((4,)), dma((6,)), dma((3, 2)), dma((44,)), dma((44,)),
        dma((2, 4, 2)), dma((2, 4, 2)), dma((2, 4, 2)), dma((2, 4, 2)),
        dma((2, 4, 3)), dma((2, 4, 3)), dma((4, 2, 2)), dma((2, 4, 2)),
        dma((2,)), dma((2,)), dma((2, 2)), dma((2,)),
    ]
    shapes = (
        jax.ShapeDtypeStruct((2, 512, 256), BF16),
        jax.ShapeDtypeStruct((2, 512, 256), BF16),
        jax.ShapeDtypeStruct((54, 128), F32),
    )
    anywhere = pl.BlockSpec(memory_space=pl.ANY)
    made = pl.pallas_call(
        kernel,
        out_shape=shapes,
        in_specs=[anywhere] * 2 + [vmem] * 5 + [anywhere],
        out_specs=(anywhere, anywhere, vmem),
        scratch_shapes=scratch,
        compiler_params=pltpu.CompilerParams(
            collective_id=0, has_side_effects=True, vmem_limit_bytes=60 * 2**20
        ),
        name="layer",
    )(
        features[0], cotangent[0], active[0], neighbours[0], cond[0],
        gamma.reshape(1, 256), beta.reshape(1, 256), weight.reshape(9, 768, 256),
    )
    output, feature_grad, weight_grad = pl.pallas_call(
        hand_out, out_shape=shapes, in_specs=[anywhere] * 3, out_specs=(anywhere,) * 3,
        scratch_shapes=[pltpu.VMEM(v.shape, v.dtype) for v in shapes] + [dma((3, 2)), dma((3, 2))],
        compiler_params=pltpu.CompilerParams(vmem_limit_bytes=60 * 2**20), name="hand_out",
    )(*made)
    return output[None], feature_grad[None], weight_grad.reshape(-1)


def solution(mesh):
    whole = P("dp", "bricks", None, None)
    rows = P("dp", "bricks", None)
    return jax.shard_map(
        on_device, mesh=mesh, in_specs=(whole, rows, rows, rows, P(), P(), P(), whole),
        out_specs=(whole, whole, P(("dp", "bricks"))), check_vma=False,
    )
```

```python
import functools

import jax
import jax.numpy as jnp
from jax import lax
from jax.experimental import pallas as pl
from jax.experimental.pallas import tpu as pltpu
from jax.sharding import PartitionSpec as P

MESH = pl.DeviceIdType.MESH
F32 = jnp.float32
BF16 = jnp.bfloat16
EPSILON = 1e-05
BIG = 1e30
LIMIT = 1e29
LAYERS = 64
ROWS = 3456
CUTS = (0, 2, 3, 4, 5)
LEAD = 384


def moved(index, stride, size, step):
    digit = (index // stride) % size
    return index + ((digit + step) % size - digit) * stride


def block_sum(v):
    return jnp.sum(v.reshape(v.shape[0] // 8, 8, v.shape[1]), axis=0)


def column_sum(v):
    return jnp.sum(v, axis=0, keepdims=True)


def packet(*rows):
    place = lax.broadcasted_iota(jnp.int32, (8, 256), 0)
    out = jnp.zeros((8, 256), F32)
    for i, row in enumerate(rows):
        out = jnp.where(place == i, row, out)
    return out


def pooled(parts):
    count = sum(p[2:3] for p in parts)
    first = sum(p[0:1] for p in parts)
    mean = first / jnp.maximum(count, 1.0)
    second = sum(p[1:2] for p in parts)
    for p in parts:
        apart = p[0:1] / jnp.maximum(p[2:3], 1.0) - mean
        second = second + p[2:3] * apart * apart
    return packet(first, second, count)


def group_sum(row):
    v = jnp.broadcast_to(row, (8, 256))
    lane = lax.broadcasted_iota(jnp.int32, (8, 256), 1)
    for step in (1, 2, 4):
        up = pltpu.roll(v, 256 - step, 1)
        down = pltpu.roll(v, step, 1)
        v = v + jnp.where((lane & step) == 0, up, down)
    return v[0:1]


def kernel(
    feat_hbm, cot_hbm, act, nbr, cond, gamma_in, beta_in, w_hbm,
    out, fgrad, wgrad,
    feat, cot, fs, zs, face_f, face_z, conds, conds_e, nbv, nbs,
    w_fwd, w_back, hz, zz, wg, part, r1, r2, r3, zr,
    acc_f, acc_b, sg_s, outs, grads,
    own, got1, got2, back1, back2,
    w_sem, nb_sem, core_s, core_r, edge_s, edge_r, st_s, st_r, rs1_s, rs1_r, rs2_s, rs2_r, rs3_s, rs3_r, z_s, z_r,
    res_s, res_r, in_sem, out_sem,
):
    d = lax.axis_index("dp")
    b = lax.axis_index("bricks")
    c = b % 2
    layer = b // 2
    xm = (b // 8) % 4
    ym = (b // 2) % 4
    hm = b // 32
    after0 = ((layer + 1) % LAYERS) * 2
    before1 = ((layer + LAYERS - 1) % LAYERS) * 2 + 1
    beside = jnp.where(c == 0, (layer + LAYERS - 1) % LAYERS, (layer + 1) % LAYERS) * 2

    def copy(src, dst, ssem, rsem, dev):
        return pltpu.make_async_remote_copy(
            src_ref=src, dst_ref=dst, send_sem=ssem, recv_sem=rsem, device_id=dev, device_id_type=MESH
        )

    w_copy = pltpu.make_async_copy(w_hbm, w_fwd, w_sem)

    barrier = pltpu.get_barrier_semaphore()
    other = b + 1 - 2 * c
    near = []
    for j in range(4):
        up = moved(b, 32, 4, j)
        near += [up, up + 1 - 2 * c]
    across = [moved(moved(b, 8, 4, j), 2, 4, i) for j in range(4) for i in range(4)]
    partners = [{"dp": 1 - d, "bricks": dev} for dev in near]
    partners += [{"bricks": dev} for dev in near[1:] + across[1:]]
    partners += [{"bricks": after0}, {"bricks": before1}, {"bricks": beside}, {"bricks": beside + 1}]
    for dev in partners:
        pl.semaphore_signal(barrier, inc=1, device_id=dev, device_id_type=MESH)
    in_copies = []
    for k, (src, dst) in enumerate(((feat_hbm, feat), (cot_hbm, cot))):
        for s in range(2):
            cp = pltpu.make_async_copy(src.at[s], dst.at[s], in_sem.at[s, k])
            cp.start()
            in_copies.append(cp)

    rows = [act[s : s + 1, 128 * j : 128 * j + 128] for s in range(2) for j in range(4)]
    flags = jnp.concatenate(rows, axis=0).astype(F32)
    count = jnp.sum(jnp.sum(flags, axis=1, keepdims=True), axis=0, keepdims=True)
    flags_t = flags.T
    def active_rows(s, j):
        return jnp.broadcast_to(flags_t[:, 4 * s + j : 4 * s + j + 1], (128, 256)) > 0.5

    shift = None
    first = jnp.zeros((8, 256), F32)
    second = jnp.zeros((8, 256), F32)
    for s in range(2):
        in_copies[s].wait()
        for j in range(4):
            m = active_rows(s, j)
            f = feat[s, pl.ds(128 * j, 128), :].astype(F32)
            if shift is None:
                held = column_sum(block_sum(jnp.where(m, 1.0, 0.0)))
                shift = column_sum(block_sum(jnp.where(m, f, 0.0))) / jnp.maximum(held, 1.0)
            apart = jnp.where(m, f - shift, 0.0)
            first = first + block_sum(apart)
            second = second + block_sum(apart * apart)
    first = column_sum(first)
    second = column_sum(second) - first * first / jnp.maximum(count, 1.0)
    first = first + count * shift
    own[0] = packet(first, second, jnp.broadcast_to(count, (1, 256)))
    pl.semaphore_wait(barrier, len(partners))

    def spread_start(stage, devices, boxes, base):
        sent = []
        for j, dev in enumerate(devices):
            cp = copy(own.at[stage], boxes.at[j], st_s.at[base + j], st_r.at[base + j], {"bricks": dev})
            cp.start()
            sent.append(cp)
        return sent

    def spread_end(sent, stage, boxes):
        for cp in sent:
            cp.wait()
        return [own[stage]] + [boxes[j] for j in range(len(sent))]

    sent = spread_start(0, near[1:], got1, 0)

    in_copies[2].wait()
    in_copies[3].wait()
    w_copy.start()
    for s in range(2):
        for j in range(4):
            at = pl.ds(128 * j, 128)
            m = active_rows(s, j)
            fs[2 * c + s, at, :] = jnp.where(m, feat[s, at, :].astype(F32), BIG).astype(BF16)
            zs[2 * c + s, at, :] = jnp.where(m, cot[s, at, :].astype(F32), 0.0).astype(BF16)
    nbv[c] = jnp.zeros((8, 128), jnp.int32)
    nbv[c, 0:2, 0:27] = nbr[...]
    for s in range(2):
        conds[2 * c + s] = jnp.broadcast_to(cond[s : s + 1, :].astype(F32), (8, 256))
    mine = pl.ds(2 * c, 2)
    core_copies = [
        copy(r.at[i], r.at[i], core_s.at[k], core_r.at[k], {"bricks": other})
        for k, (r, i) in enumerate(((nbv, c), (zs, mine), (fs, mine), (conds, mine)))
    ]
    for cp in core_copies:
        cp.start()
    edge_copies = []
    for k, (src, dst, up, down) in enumerate((
        (zs, face_z, pl.ds(448, 64), pl.ds(0, 64)),
        (fs, face_f, pl.ds(448, 64), pl.ds(0, 64)),
        (conds, conds_e, pl.ds(0, 8), pl.ds(0, 8)),
    )):
        for way, (at, dev) in enumerate(((up, after0), (down, before1))):
            cp = copy(
                src.at[mine, at], dst.at[mine], edge_s.at[2 * k + way], edge_r.at[k, c], {"bricks": dev}
            )
            cp.start()
            edge_copies.append(cp)

    def edge_wait(k, dst):
        for core in range(2):
            got = dst.at[pl.ds(2 * core, 2)]
            copy(got, got, edge_s.at[2 * k], edge_r.at[k, core], {"bricks": other}).wait_recv()

    for grid in (hz, zz):
        grid[:, 0:16, :] = jnp.zeros((10, 16, 768), BF16)
        grid[:, 272:288, :] = jnp.zeros((10, 16, 768), BF16)
    fs[4] = jnp.full((512, 256), BIG, BF16)
    zs[4] = jnp.zeros((512, 256), BF16)
    face_f[4] = jnp.full((64, 256), BIG, BF16)
    face_z[4] = jnp.zeros((64, 256), BF16)
    conds[4] = jnp.zeros((8, 256), F32)
    conds_e[4] = jnp.zeros((8, 256), F32)
    wg[pl.ds(LEAD + ROWS, 8), :] = jnp.zeros((8, 256), F32)

    w_copy.wait()

    def turn(g, carry):
        for e in range(3):
            w_back[g, pl.ds(256 * e, 256), :] = w_fwd[8 - g, pl.ds(256 * (2 - e), 256), :].T
        return carry

    lax.fori_loop(0, 9, turn, 0)

    core_copies[0].wait()
    nb_copy = pltpu.make_async_copy(nbv, nbs, nb_sem)
    nb_copy.start()
    nb_copy.wait()
    cy, cz, src, src_e = [], [], [], []
    here = []
    for j in range(4):
        def entry(k):
            return nbs[j // 2, j % 2, k]

        low_y = functools.reduce(jnp.maximum, [entry(9 * a + e) for a in range(3) for e in range(3)])
        low_z = functools.reduce(jnp.maximum, [entry(9 * a + 3 * e) for a in range(3) for e in range(3)])
        cy.append(jnp.where(low_y >= 0, 1, 0))
        cz.append(jnp.where(low_z >= 0, 1, 0))
        here.append(entry(13) >= 0)
    for q in range(4):
        qy, qz = q // 2, q % 2
        at, at_e = jnp.int32(4), jnp.int32(4)
        for j in range(4):
            at = jnp.where(here[j] & (cy[j] == qy) & (cz[j] == qz), j, at)
            t = nbs[j // 2, j % 2, 18 * c + 3 * (qy + 1 - cy[j]) + (qz + 1 - cz[j])]
            at_e = jnp.where(t >= 0, t & 3, at_e)
        src.append(at)
        src_e.append(at_e)

    zi = lax.broadcasted_iota(jnp.int32, (128, 256), 0) & 15

    def joined(left, right):
        pair = [v.reshape(8, 8, 256) for v in (left, right)]
        return jnp.concatenate(pair, axis=1).reshape(128, 256)

    def lay(grid, plane, half, v):
        at = pl.ds(16 + 128 * half, 128)
        grid[plane, at, 0:256] = jnp.where(zi == 0, 0.0, pltpu.roll(v, 1, 0)).astype(BF16)
        grid[plane, at, 256:512] = v.astype(BF16)
        grid[plane, at, 512:768] = jnp.where(zi == 15, 0.0, pltpu.roll(v, 127, 0)).astype(BF16)

    edge_plane = 9 * c

    core_copies[1].wait()

    def lay_z(x, carry):
        for half in range(2):
            at = pl.ds(pl.multiple_of(64 * x, 64), 64)
            v = joined(*[zs[src[2 * half + e], at, :].astype(F32) for e in range(2)])
            lay(zz, x + 1, half, v)
        return carry

    lax.fori_loop(0, 8, lay_z, 0)

    merged = pooled(spread_end(sent, 0, got1))
    own[1] = merged
    sent = spread_start(1, across[1:], got2, 7)

    def conv(grid, taps, acc, kx):
        planes = pl.ds(4 * c + kx, 4)
        lhs = jnp.concatenate([grid[planes, 16 * e : 16 * e + 256, :].reshape(1024, 768) for e in range(3)], axis=1)
        rhs = taps[3 * kx : 3 * kx + 3].reshape(2304, 256)
        made = jnp.dot(lhs, rhs, preferred_element_type=F32).reshape(4, 2, 8, 2, 8, 256)
        acc[...] = made if kx == 1 else acc[...] + made

    conv(zz, w_back, acc_b, 1)
    edge_wait(0, face_z)
    for half in range(2):
        lay(zz, edge_plane, half, joined(*[face_z[src_e[2 * half + e]].astype(F32) for e in range(2)]))
    conv(zz, w_back, acc_b, 0)
    conv(zz, w_back, acc_b, 2)

    merged = pooled(spread_end(sent, 1, got2))
    total = merged[2:3]
    first, second = merged[0:1], merged[1:2]
    total_g = 8.0 * total
    mean = group_sum(first) / total_g
    apart = first / total - mean
    var = group_sum(second + total * apart * apart) / total_g
    inv_std = lax.rsqrt(var + EPSILON)
    gamma = gamma_in[...]
    beta = beta_in[...]
    slope = inv_std * gamma

    for cp in core_copies[2:]:
        cp.wait()
    edge_wait(1, face_f)
    edge_wait(2, conds_e)

    def activation(raw, shift):
        f = raw.astype(F32)
        m = f < LIMIT
        f = jnp.where(m, f, 0.0)
        apart = f - mean
        pre = apart * slope + (beta + shift[0:1])
        sigma = 1.0 / (1.0 + jnp.exp(-pre))
        return m, f, apart, pre, sigma

    def hidden(raw, shift):
        m, _, _, pre, sigma = activation(raw, shift)
        return jnp.where(m, pre * sigma, 0.0)

    def lay_h(x, carry):
        for half in range(2):
            at = pl.ds(pl.multiple_of(64 * x, 64), 64)
            slots = [src[2 * half + e] for e in range(2)]
            lay(hz, x + 1, half, joined(*[hidden(fs[j, at, :], conds[j]) for j in slots]))
        return carry

    lax.fori_loop(0, 8, lay_h, 0)
    for half in range(2):
        slots = [src_e[2 * half + e] for e in range(2)]
        lay(hz, edge_plane, half, joined(*[hidden(face_f[j], conds_e[j]) for j in slots]))

    def taps(low, high):
        def step(i, carry):
            g = 4 * c + i
            at = pl.ds(pl.multiple_of(g % 3 * 16, 16), 256)
            lhs = hz[pl.ds(g // 3, 8), at, :].reshape(2048, 768)
            center = zz[1:9, 16:272, 256:512].reshape(2048, 256)
            wg[pl.ds(pl.multiple_of(LEAD * (1 - c) + 768 * i, 128), 768), :] = lax.dot_general(
                lhs, center, (((0,), (0,)), ((), ())), preferred_element_type=F32
            )
            return carry

        lax.fori_loop(low, high, step, 0)

    way = ((8, 2), (2, 8))
    place = ((xm, ym), (ym, xm))

    def deal(h):
        def step(x, carry):
            base = pl.multiple_of(LEAD + 864 * h + 216 * x, 8)
            for y in range(4):
                low = 54 * y // 8 * 8
                v = wg[pl.ds(base + low, 64), :][54 * y - low : 54 * y - low + 54]
                part[0, x, h, y] = v[:, 0:128]
                part[1, y, h, x] = v[:, 128:256]
            return carry

        lax.fori_loop(0, 4, step, 0)

    live = {}

    def first_start(h):
        for k in range(2):
            a = place[k][0]
            for e, step in ((0, 1), (1, 3)):
                cp = copy(
                    part.at[k, (a + 2) % 4, h, pl.ds(2 * e, 2)], r1.at[k, h, e],
                    rs1_s.at[k, h, e], rs1_r.at[k, h, e], {"bricks": moved(b, way[k][0], 4, step)},
                )
                cp.start()
                live[1, k, h, e] = cp

    def second_start(h):
        for k in range(2):
            a = place[k][0]
            for e, step in ((0, 1), (1, 3)):
                live[1, k, h, e].wait()
                to = (a + step) % 4
                part[k, to, h, pl.ds(2 * e, 2)] += r1[k, h, e]
                cp = copy(
                    part.at[k, to, h], r2.at[k, h, e], rs2_s.at[k, h, e], rs2_r.at[k, h, e],
                    {"bricks": moved(b, way[k][0], 4, step)},
                )
                cp.start()
                live[2, k, h, e] = cp

    def third_start(h):
        for k in range(2):
            a, at = place[k]
            for e in range(2):
                live[2, k, h, e].wait()
            part[k, a, h] += r2[k, h, 0] + r2[k, h, 1]
            for j in range(1, 4):
                cp = copy(
                    part.at[k, a, h, (at + j) % 4], r3.at[k, h, j - 1], rs3_s.at[k, h, j - 1], rs3_r.at[k, h, j - 1],
                    {"bricks": moved(b, way[k][1], 4, j)},
                )
                cp.start()
                live[3, k, h, j] = cp

    side = jnp.where(c == d, 0, 1)

    def window(core):
        return pl.ds(pl.multiple_of(24 * core, 8), 30)

    def to_self(h):
        return (c == d) & (hm == h)

    def z_copies(h):
        one, two = [], []
        for k in range(2):
            a, at = place[k]
            base = b % 32 + 32 * h
            for group, core, dev in ((one, 1 - c, base + 1 - 2 * c), (two, c, base)):
                group.append(copy(
                    part.at[k, a, h, at, window(core)], zr.at[side, hm, k],
                    z_s.at[h, len(group), k], z_r.at[side, hm, k], {"dp": c, "bricks": dev},
                ))
        return one, two

    def z_start(h):
        for k in range(2):
            a, at = place[k]
            for j in range(1, 4):
                live[3, k, h, j].wait()
            part[k, a, h, at] += r3[k, h, 0] + r3[k, h, 1] + r3[k, h, 2]
        one, two = z_copies(h)
        for cp in one:
            cp.start()

        @pl.when(jnp.logical_not(to_self(h)))
        def _():
            for cp in two:
                cp.start()

        @pl.when(to_self(h))
        def _():
            for k in range(2):
                a, at = place[k]
                zr[0, h, k] = part[k, a, h, at, window(c), :]

    def z_end():
        for h in range(4):
            one, two = z_copies(h)
            for cp in one:
                cp.wait_send()

            @pl.when(jnp.logical_not(to_self(h)))
            def _():
                for cp in two:
                    cp.wait_send()
                for k in range(2):
                    copy(zr.at[0, h, k], zr.at[0, h, k], z_s.at[h, 0, k], z_r.at[0, h, k], {"bricks": other}).wait_recv()

            for k in range(2):
                copy(zr.at[1, h, k], zr.at[1, h, k], z_s.at[h, 0, k], z_r.at[1, h, k], {"bricks": other}).wait_recv()
        for k in range(2):
            v = sum(zr[e, h, k] for e in range(2) for h in range(4))
            wgrad[pl.ds(k, 27, stride=2), :] = jnp.where(c == 0, v[0:27], v[3:30])

    def slot_block(j, plane):
        at = pl.ds(pl.multiple_of(256 * c + 64 * plane, 64), 64)
        return at, activation(fs[j, at, :], conds[j])

    def back_pass(plane, carry):
        one, two = carry
        for j in range(4):
            at, (m, f, apart, pre, sigma) = slot_block(j, plane)
            back = acc_b[plane, cy[j], :, cz[j]].reshape(64, 256)
            sg = jnp.where(m, gamma * back * sigma * (1.0 + pre * (1.0 - sigma)), 0.0)
            sg_s[j, plane] = sg
            one = one + block_sum(sg)
            two = two + block_sum(sg * (apart * inv_std))
        return one, two

    def back_start():
        zero = jnp.zeros((8, 256), F32)
        one, two = lax.fori_loop(0, 4, back_pass, (zero, zero))
        own[2] = packet(column_sum(one), column_sum(two))
        return spread_start(2, across[1:], back1, 22)

    def out_pass(plane, carry):
        for j in range(4):
            at = pl.ds(pl.multiple_of(256 * c + 64 * plane, 64), 64)
            f = fs[j, at, :].astype(F32)
            made = acc_f[plane, cy[j], :, cz[j]].reshape(64, 256)
            outs[j, at, :] = jnp.where(f < LIMIT, f + made, 0.0).astype(BF16)
        return carry

    theirs = pl.ds(2 - 2 * c, 2)
    half_rows = pl.ds(pl.multiple_of(256 * c, 256), 256)

    def hand_over(ref, k):
        piece = ref.at[theirs, half_rows]
        cp = copy(piece, piece, res_s.at[k], res_r.at[k], {"bricks": other})
        cp.start()
        return cp

    def grad_pass(grad_mean, cross_mean, plane, carry):
        for j in range(4):
            at = pl.ds(pl.multiple_of(256 * c + 64 * plane, 64), 64)
            f = fs[j, at, :].astype(F32)
            x_hat = (f - mean) * inv_std
            v = inv_std * (sg_s[j, plane] - grad_mean - x_hat * cross_mean) + zs[j, at, :].astype(F32)
            grads[j, at, :] = jnp.where(f < LIMIT, v, 0.0).astype(BF16)
        return carry

    for h in range(4):
        taps(CUTS[h], CUTS[h + 1])
        deal(h)
        first_start(h)
        if h == 0:
            sent = back_start()
        if 1 <= h <= 2:
            second_start(h - 1)
    own[3] = sum(spread_end(sent, 2, back1))
    sent = spread_start(3, near[1:], back2, 37)
    conv(hz, w_fwd, acc_f, 1)
    third_start(0)
    second_start(2)
    conv(hz, w_fwd, acc_f, 0)
    third_start(1)
    second_start(3)
    third_start(2)
    sums = sum(spread_end(sent, 3, back2))
    grad_mean = group_sum(sums[0:1]) / total_g
    cross_mean = group_sum(sums[1:2]) / total_g
    lax.fori_loop(0, 4, functools.partial(grad_pass, grad_mean, cross_mean), 0)
    grad_copy = hand_over(grads, 1)
    z_start(0)
    conv(hz, w_fwd, acc_f, 2)
    lax.fori_loop(0, 4, out_pass, 0)
    out_copy = hand_over(outs, 0)
    third_start(3)
    z_start(1)
    z_start(2)
    stores = []
    for k, (cp, ref, to) in enumerate(((out_copy, outs, out), (grad_copy, grads, fgrad))):
        cp.wait()
        stores.append(pltpu.make_async_copy(ref.at[mine], to, out_sem.at[k]))
        stores[k].start()
    z_start(3)
    for cp in edge_copies:
        cp.wait_send()
    for cp in stores:
        cp.wait()
    z_end()


def hand_out(*refs):
    sources, targets, held, sem_in, sem_out = refs[:3], refs[3:6], refs[6:9], refs[9], refs[10]
    steps = []
    for i in range(3):
        rows = sources[i].shape[0]
        for k in range(1 if i == 2 else rows):
            at = pl.ds(0, rows) if i == 2 else pl.ds(k, 1)
            steps.append((
                pltpu.make_async_copy(sources[i].at[at], held[i].at[at], sem_in.at[i, k]),
                pltpu.make_async_copy(held[i].at[at], targets[i].at[at], sem_out.at[i, k]),
            ))
    for load, _ in steps:
        load.start()
    for load, store in steps:
        load.wait()
        store.start()
    for _, store in steps:
        store.wait()


def on_device(features, active, neighbours, cond, gamma, beta, weight, cotangent):
    vmem = pl.BlockSpec(memory_space=pltpu.VMEM)
    dma = pltpu.SemaphoreType.DMA
    scratch = [
        pltpu.VMEM((2, 512, 256), BF16),
        pltpu.VMEM((2, 512, 256), BF16),
        pltpu.VMEM((5, 512, 256), BF16),
        pltpu.VMEM((5, 512, 256), BF16),
        pltpu.VMEM((5, 64, 256), BF16),
        pltpu.VMEM((5, 64, 256), BF16),
        pltpu.VMEM((5, 8, 256), F32),
        pltpu.VMEM((5, 8, 256), F32),
        pltpu.VMEM((2, 8, 128), jnp.int32),
        pltpu.SMEM((2, 8, 128), jnp.int32),
        pltpu.VMEM((9, 768, 256), BF16),
        pltpu.VMEM((9, 768, 256), BF16),
        pltpu.VMEM((10, 288, 768), BF16),
        pltpu.VMEM((10, 288, 768), BF16),
        pltpu.VMEM((LEAD + 3840, 256), F32),
        pltpu.VMEM((2, 4, 4, 4, 54, 128), F32),
        pltpu.VMEM((2, 4, 2, 2, 54, 128), F32),
        pltpu.VMEM((2, 4, 2, 4, 54, 128), F32),
        pltpu.VMEM((2, 4, 3, 54, 128), F32),
        pltpu.VMEM((2, 4, 2, 30, 128), F32),
        pltpu.VMEM((4, 2, 8, 2, 8, 256), F32),
        pltpu.VMEM((4, 2, 8, 2, 8, 256), F32),
        pltpu.VMEM((4, 4, 64, 256), F32),
        pltpu.VMEM((4, 512, 256), BF16),
        pltpu.VMEM((4, 512, 256), BF16),
        pltpu.VMEM((4, 8, 256), F32),
        pltpu.VMEM((7, 8, 256), F32),
        pltpu.VMEM((15, 8, 256), F32),
        pltpu.VMEM((15, 8, 256), F32),
        pltpu.VMEM((7, 8, 256), F32),
        dma, dma, dma((4,)), dma((4,)), dma((6,)), dma((3, 2)), dma((44,)), dma((44,)),
        dma((2, 4, 2)), dma((2, 4, 2)), dma((2, 4, 2)), dma((2, 4, 2)),
        dma((2, 4, 3)), dma((2, 4, 3)), dma((4, 2, 2)), dma((2, 4, 2)),
        dma((2,)), dma((2,)), dma((2, 2)), dma((2,)),
    ]
    shapes = (
        jax.ShapeDtypeStruct((2, 512, 256), BF16),
        jax.ShapeDtypeStruct((2, 512, 256), BF16),
        jax.ShapeDtypeStruct((54, 128), F32),
    )
    anywhere = pl.BlockSpec(memory_space=pl.ANY)
    made = pl.pallas_call(
        kernel,
        out_shape=shapes,
        in_specs=[anywhere] * 2 + [vmem] * 5 + [anywhere],
        out_specs=(anywhere, anywhere, vmem),
        scratch_shapes=scratch,
        compiler_params=pltpu.CompilerParams(
            collective_id=0, has_side_effects=True, vmem_limit_bytes=60 * 2**20
        ),
        name="layer",
    )(
        features[0], cotangent[0], active[0], neighbours[0], cond[0],
        gamma.reshape(1, 256), beta.reshape(1, 256), weight.reshape(9, 768, 256),
    )
    output, feature_grad, weight_grad = pl.pallas_call(
        hand_out, out_shape=shapes, in_specs=[anywhere] * 3, out_specs=(anywhere,) * 3,
        scratch_shapes=[pltpu.VMEM(v.shape, v.dtype) for v in shapes] + [dma((3, 2)), dma((3, 2))],
        compiler_params=pltpu.CompilerParams(vmem_limit_bytes=60 * 2**20), name="hand_out",
    )(*made)
    return output[None], feature_grad[None], weight_grad.reshape(-1)


def solution(mesh):
    whole = P("dp", "bricks", None, None)
    rows = P("dp", "bricks", None)
    return jax.shard_map(
        on_device, mesh=mesh, in_specs=(whole, rows, rows, rows, P(), P(), P(), whole),
        out_specs=(whole, whole, P(("dp", "bricks"))), check_vma=False,
    )
```
